32 devices in a mesh: dp: 32 (over z, y, x, core).
Axes of the slice: x: 2, y: 2, z: 4, core: 2. Of those that a mesh axis runs over, the one named last changes fastest.
Arguments:
- step_index: int32 [1], replicated, may hold values from 0 to 63
- dest: int32 [2, 8192, 1], P(None, 'dp'), may hold values from 0 to 31; in each aligned block of 256 rows (0 to 255, 256 to 511, ..., all dimensions but the last counted through in order) at most 16 rows name the same one
- tokens: bfloat16 [2, 8192, 1024], P(None, 'dp'), may hold values from -6 to 6
- params: float32 [32768, 1024], P('dp'), may hold values from -0.1875 to 0.1875
- trackers: float32 [32768, 1024], P('dp'), may hold values from -4 to 4
- old_grads: float32 [32768, 1024], P('dp'), may hold values from -4 to 4
- key_weight: bfloat16 [1024, 1024], replicated, may hold values from -0.1875 to 0.1875
- latents: bfloat16 [128, 1024], replicated, may hold values from -6 to 6
- targets: float32 [4096, 1024], P('dp'), may hold values from -6 to 6
Outputs:
- new_params: float32 [32768, 1024], P('dp')
- new_trackers: float32 [32768, 1024], P('dp')
The draws below stay inside these ranges and needn't reach their ends.
Inputs may be any that keep to these rules, and one draw needn't show every extreme that they name: `dest`: in each step no trainer receives more than 16 rows from the rows of one device, and that bound is reached; every trainer receives some row.
All inputs are finite; a program needn't handle non-finite values.
Results may differ from the reference program's by a relative error of at most 0.012.
Values may be sent and summed in bfloat16 or wider, within the bound.
No kernel may reach another device: no remote copies, remote signals or barrier semaphores. Data moves between devices by JAX's collectives and lax.ppermute only.
A program may use at most 128 MiB of HBM per device.

```python
import math
import jax
import jax.numpy as jnp
import numpy as np
from jax import lax

D = 1024
HEADS = 16
HEAD_DIM = 64
LAT = 128
ROWS_DEV = 256
STEPS = 2
CAP = 16
WINDOW = 512
TOKENS = 8192
N_DP = 32


def levels(own_key, extent, shards, least, largest):
    def one(position, parts):
        steps = jax.random.uniform(jax.random.fold_in(jax.random.fold_in(own_key, 6), position), (parts,), jnp.float32, least / len(shards), largest / len(shards))
        return jnp.repeat(jnp.exp(steps), extent[position] // parts).reshape((-1,) + (1,) * (len(extent) - position - 1))

    gain = one(*shards[0])
    for cut in shards[1:]:
        gain = gain * one(*cut)
    return gain


def routed_block(rng, own, number, rows, number_of, top, limit, lean):
    ranking = jax.random.permutation(rng, number_of)
    packed, ordinary = shares(number_of, rows * top, limit, lean, True), shares(number_of, rows * top, limit, lean, False)
    places = jnp.arange(number_of)

    def named(lengths, offset_by):
        used = int((lengths > 0).sum())
        fixed = max(1, used // 4)
        moved = fixed + (places - fixed + offset_by * (used - fixed)) % max(1, number_of - fixed)
        return jnp.zeros((number_of,), jnp.int32).at[ranking[jnp.where(places < fixed, places, moved)]].set(jnp.asarray(lengths, jnp.int32))

    lengths = jnp.where(number % 4 == 0, named(packed, number // 4), named(ordinary, number - number // 4 - 1))
    mixed = jax.random.permutation(jax.random.fold_in(own, 3), number_of)
    donor, receiver = mixed[0:number_of // 2 * 2:2], mixed[1:number_of // 2 * 2:2]
    margin = jnp.minimum(lengths[donor] - 1, limit - lengths[receiver]) // 2
    margin = jnp.where((donor == ranking[0]) | (receiver == ranking[0]) | (lengths[receiver] == 0), 0, jnp.maximum(margin, 0))
    moved = jax.random.randint(jax.random.fold_in(own, 4), (number_of // 2,), 0, 1 << 20) % (margin + 1)
    lengths = lengths.at[donor].add(-moved).at[receiver].add(moved)
    items = jnp.searchsorted(jnp.cumsum(lengths), jnp.arange(rows * top), side="right").astype(jnp.int32)
    listing = items.reshape(top, rows).T
    listing = listing[jax.random.permutation(jax.random.fold_in(own, 1), rows)]
    offset_by = jax.random.randint(jax.random.fold_in(own, 2), (rows, 1), 0, top)
    return jnp.take_along_axis(listing, (jnp.arange(top)[None, :] + offset_by) % top, axis=1)


def shares(amount, total, limit, slope, full):
    weights = [(1 << 20) // math.isqrt(grade ** slope) + 1 for grade in range(1, amount + 1)]
    largest = limit if full else min(limit, max(-(-total // amount), total * weights[0] // sum(weights)))
    least = 1 if total - largest >= amount - 1 else 0
    holding, surplus = [largest] + [least] * (amount - 1), total - largest - least * (amount - 1)
    while surplus > 0:
        candidates = [i for i in range(1, amount) if holding[i] < largest] or [i for i in range(1, amount) if holding[i] < limit]
        pool, remaining = sum([weights[i] for i in candidates]), surplus
        for i in candidates:
            more = min(limit - holding[i], max(1, remaining * weights[i] // pool), surplus)
            holding[i] = holding[i] + more
            surplus = surplus - more
    return np.array(holding)


def scatter_about(stream_key, shape, deviation, limit, cuts=(), kind=jnp.bfloat16):
    result = deviation * jax.random.normal(stream_key, shape, jnp.float32)
    if cuts:
        result = result * levels(stream_key, shape, cuts, -0.22, 0.18)
    return jnp.clip(result, -limit, limit).astype(kind)


def setup_inputs(seed: int = 0) -> dict:
    arg_keys = jax.random.split(jax.random.key(seed), 10)
    step_index = jax.random.randint(arg_keys[0], (1,), 0, 64).astype(jnp.int32)
    dest_keys = jax.random.split(jax.random.fold_in(arg_keys[1], 1), STEPS * TOKENS // ROWS_DEV)
    dest_turns = jax.random.permutation(jax.random.fold_in(arg_keys[1], 3), STEPS * TOKENS // ROWS_DEV)
    dest = jax.vmap(lambda own, number: routed_block(jax.random.fold_in(arg_keys[1], 2), own, number, ROWS_DEV, N_DP, 1, CAP, 2))(dest_keys, dest_turns).reshape((STEPS, TOKENS, 1))
    tokens = scatter_about(arg_keys[2], (STEPS, TOKENS, D), 1.0, 6.0, ((1, 32),))
    params = scatter_about(arg_keys[3], (N_DP * D, D), D ** -0.5, 0.1875, ((0, 32),), jnp.float32)
    trackers = scatter_about(arg_keys[4], (N_DP * D, D), 0.5, 4.0, ((0, 32),), jnp.float32)
    old_grads = scatter_about(arg_keys[5], (N_DP * D, D), 0.5, 4.0, ((0, 32),), jnp.float32)
    key_weight = scatter_about(arg_keys[6], (D, D), D ** -0.5, 0.1875)
    latents = scatter_about(arg_keys[7], (LAT, D), 1.0, 6.0)
    targets = scatter_about(arg_keys[8], (N_DP * LAT, D), 1.0, 6.0, ((0, 32),), jnp.float32)
    return {"step_index": step_index, "dest": dest, "tokens": tokens, "params": params, "trackers": trackers, "old_grads": old_grads, "key_weight": key_weight, "latents": latents, "targets": targets}


def local_grad(weight, rows, live, key_weight, latents, target):
    win = rows.shape[0]
    keys = jnp.dot(rows, key_weight, preferred_element_type=jnp.float32).astype(jnp.bfloat16)
    values = jnp.dot(rows, weight.astype(jnp.bfloat16), preferred_element_type=jnp.float32).astype(jnp.bfloat16)
    queries = latents.astype(jnp.float32).reshape(LAT, HEADS, HEAD_DIM)
    keyed = keys.astype(jnp.float32).reshape(win, HEADS, HEAD_DIM)
    scores = jnp.einsum('lhd,jhd->hlj', queries, keyed) / jnp.sqrt(jnp.float32(HEAD_DIM))
    attn = (jax.nn.sigmoid(scores - 3.5) * live[None, None, :]).astype(jnp.bfloat16)
    attf = attn.astype(jnp.float32)
    out = jnp.einsum('hlj,jhd->lhd', attf, values.astype(jnp.float32).reshape(win, HEADS, HEAD_DIM)).reshape(LAT, D)
    resid = ((out - target) / 16.0).astype(jnp.bfloat16)
    dvalues = jnp.einsum('hlj,lhd->jhd', attf, resid.astype(jnp.float32).reshape(LAT, HEADS, HEAD_DIM))
    dvalues = dvalues.reshape(win, D).astype(jnp.bfloat16)
    return lax.dot_general(rows, dvalues, (((0,), (0,)), ((), ())), preferred_element_type=jnp.float32)

def reference(step_index, dest, tokens, params, trackers, old_grads, key_weight, latents, targets):
    logn = int(N_DP).bit_length() - 1
    params_all = params.reshape(N_DP, D, D)
    track_all = trackers.reshape(N_DP, D, D)
    grads_all = old_grads.reshape(N_DP, D, D)
    target_all = targets.reshape(N_DP, LAT, D)
    trainer_ids = jnp.arange(N_DP, dtype=jnp.int32)
    for step in range(STEPS):
        bit = (step_index[0] + step) % logn
        partner = jnp.bitwise_xor(trainer_ids, jnp.left_shift(jnp.int32(1), bit.astype(jnp.int32))).astype(jnp.int32)
        new_params = 0.5 * (params_all + params_all[partner]) - 0.05 * track_all
        mixed_track = 0.5 * (track_all + track_all[partner])
        owner = dest[step, :, 0]
        order = jnp.argsort(owner, stable=True)
        sorted_rows = jnp.concatenate([tokens[step][order], jnp.zeros((WINDOW, D), jnp.bfloat16)], axis=0)
        counts = lax.optimization_barrier(jnp.sum((owner[:, None] == trainer_ids[None, :]).astype(jnp.int32), axis=0))
        starts = (jnp.cumsum(counts) - counts).astype(jnp.int32)

        def one(idx):
            rows = lax.dynamic_slice(sorted_rows, (starts[idx], jnp.int32(0)), (WINDOW, D))
            live = (jnp.arange(WINDOW, dtype=jnp.int32) < counts[idx]).astype(jnp.float32)
            return local_grad(new_params[idx], rows, live, key_weight, latents, target_all[idx])
        new_grads = lax.map(one, trainer_ids)
        track_all = mixed_track + new_grads - grads_all
        grads_all = new_grads
        params_all = new_params
    return (params_all.reshape(N_DP * D, D), track_all.reshape(N_DP * D, D))
```

```python
from functools import partial

import jax
import jax.numpy as jnp
from jax import lax
from jax.experimental import pallas as pl
from jax.experimental.pallas import tpu as pltpu
from jax.sharding import PartitionSpec as P

HEADS = 16
STEPS = 2
GROUPS = (4, 4, 4, 4)
ATTN_HEADS = 4
F32 = jnp.float32
BF16 = jnp.bfloat16


class Chain:
    def __init__(self):
        self.token = None
        self.held = []

    def hold(self, value):
        self.held.append(value)

    def call(self, body, name, grid, ins, outs, vmem, aliases=None, scratch=()):
        after = self.held + ([] if self.token is None else [self.token])
        self.held = []
        arrays = [a for a, _ in ins] + after
        specs = [s for _, s in ins] + [pl.BlockSpec(memory_space=pl.ANY)] * len(after)
        count_in, count_out = len(ins), len(outs)

        def kernel(*refs):
            given_out = len(arrays) + count_out
            body(*refs[:count_in], *refs[len(arrays) : given_out], *refs[given_out + 1 :])

        given = pl.pallas_call(
            kernel,
            out_shape=tuple(o for o, _ in outs) + (jax.ShapeDtypeStruct((8, 128), F32),),
            grid=grid,
            scratch_shapes=list(scratch),
            in_specs=specs,
            out_specs=tuple(s for _, s in outs) + (pl.BlockSpec(memory_space=pl.ANY),),
            input_output_aliases=dict(aliases or {}),
            compiler_params=pltpu.CompilerParams(vmem_limit_bytes=vmem * 1024 * 1024),
            cost_estimate=pl.CostEstimate(flops=1, bytes_accessed=1, transcendentals=0),
            name=name,
        )(*arrays)
        self.token = given[-1]
        return given[:-1]


BLOCK = 256
STRIP = 32


def at_block(i, size):
    return pl.ds(pl.multiple_of(i * size, size), size)


def in_strips(body, *refs):
    flat = [ref.at[0] if len(ref.shape) == 3 else ref for ref in refs]

    @pl.loop(0, flat[0].shape[0] // STRIP)
    def _(i):
        body(*[ref.at[at_block(i, STRIP), :] for ref in flat])


def shape(dims, dtype):
    return jax.ShapeDtypeStruct(dims, dtype)


def pack_body(dest_ref, tokens_ref, out_ref, *, count_dev, cap):
    owner = dest_ref[0]
    rows = owner.shape[1]
    trainer = lax.broadcasted_iota(jnp.int32, (count_dev, rows), 0)
    named = (trainer == owner).astype(F32)
    earlier = lax.broadcasted_iota(jnp.int32, (rows, rows), 0) < lax.broadcasted_iota(
        jnp.int32, (rows, rows), 1
    )
    before = jnp.dot(
        named.astype(BF16), earlier.astype(F32).astype(BF16), preferred_element_type=F32
    )
    rank = jnp.sum(named * before, axis=0, keepdims=True).astype(jnp.int32)
    where = owner * cap + rank

    @pl.loop(0, out_ref.shape[0] // BLOCK)
    def _(i):
        slot = lax.broadcasted_iota(jnp.int32, (BLOCK, rows), 0) + i * BLOCK
        chosen = (slot == where).astype(F32).astype(BF16)
        out_ref[at_block(i, BLOCK), :] = jnp.dot(
            chosen, tokens_ref[0], preferred_element_type=F32
        ).astype(BF16)


def pack_rows(chain, dest, tokens, count_dev):
    steps, rows, width = tokens.shape
    cap = 2 * rows // count_dev
    slots = count_dev * cap
    span = width
    return chain.call(
        partial(pack_body, count_dev=count_dev, cap=cap),
        "pack_rows",
        (steps, width // span),
        [
            (dest.reshape(steps, 1, rows), pl.BlockSpec((1, 1, rows), lambda k, i: (k, 0, 0))),
            (tokens, pl.BlockSpec((1, rows, span), lambda k, i: (k, 0, i))),
        ],
        [
            (
                shape((slots, steps * width), BF16),
                pl.BlockSpec((slots, span), lambda k, i: (0, k * (width // span) + i)),
            )
        ],
        vmem=16,
    )[0]


def round_body(*refs):
    def strip(src_ref, out_ref):
        out_ref[...] = src_ref[...].astype(BF16)

    in_strips(strip, *refs)


def round_columns(chain, whole, at, span, block_rows=256):
    rows = whole.shape[0]
    return chain.call(
        round_body,
        "round_columns",
        (rows // block_rows,),
        [(whole, pl.BlockSpec((block_rows, span), lambda i: (i, at)))],
        [(shape((rows, span), BF16), pl.BlockSpec((block_rows, span), lambda i: (i, 0)))],
        vmem=4,
    )[0]


def of_head(head, head_size, value):
    column = lax.broadcasted_iota(jnp.int32, value.shape, 1) // head_size
    return jnp.where(column == head, value, 0.0)


def attn_body(rows_ref, key_ref, lat_ref, attn_ref, turned_ref, *, heads, head_size):
    @pl.when(pl.program_id(1) == 0)
    def _():
        @pl.loop(0, rows_ref.shape[0] // BLOCK)
        def _(j):
            turned_ref[0, :, at_block(j, BLOCK)] = rows_ref[at_block(j, BLOCK), :].T

    latents = lat_ref[...].astype(F32)
    queries = jnp.concatenate(
        [of_head(h, head_size, latents).astype(BF16) for h in range(heads)], axis=0
    )

    @pl.loop(0, rows_ref.shape[0] // BLOCK)
    def _(j):
        keys = jnp.dot(
            rows_ref[at_block(j, BLOCK), :], key_ref[...], preferred_element_type=F32
        ).astype(BF16)
        scores = lax.dot_general(
            queries, keys, (((1,), (1,)), ((), ())), preferred_element_type=F32
        )
        scores = scores * (1.0 / head_size**0.5) - 3.5
        attn_ref[0, :, at_block(j, BLOCK)] = jax.nn.sigmoid(scores).astype(BF16)


WHOLE = pl.BlockSpec(memory_space=pltpu.VMEM)


def attention(chain, rows, key_weight, latents):
    win = rows.shape[0]
    lat, width = latents.shape
    head_size = width // HEADS
    span = ATTN_HEADS * head_size
    return chain.call(
        partial(attn_body, heads=ATTN_HEADS, head_size=head_size),
        "attention",
        (STEPS, HEADS // ATTN_HEADS),
        [
            (rows, pl.BlockSpec((win, width), lambda k, c: (0, k))),
            (key_weight, pl.BlockSpec((width, span), lambda k, c: (0, c))),
            (latents, pl.BlockSpec((lat, span), lambda k, c: (0, c))),
        ],
        [
            (
                shape((STEPS, HEADS * lat, win), BF16),
                pl.BlockSpec((1, ATTN_HEADS * lat, win), lambda k, c: (k, c, 0)),
            ),
            (
                shape((STEPS, width, win), BF16),
                pl.BlockSpec((1, width, win), lambda k, c: (k, 0, 0)),
            ),
        ],
        vmem=16,
    )


def grad_body(*refs, step, starts, heads, head_size, last):
    count = len(starts)
    rows_ref, turned_ref, attn_ref, target_ref = refs[:4]
    weight_refs = refs[4 : 4 + count]
    extra = refs[4 + count : -6]
    out_ref, weight, total, values, resid, dvalues = refs[-6:]
    win, span = values.shape
    lat = resid.shape[0] // heads
    width = weight.shape[0]
    now = pl.program_id(0)
    begin = starts[0] + now * heads

    for t in range(count):

        @pl.when(now == t)
        def _(t=t):
            @pl.loop(0, width // STRIP)
            def _(i):
                weight[at_block(i, STRIP), :] = weight_refs[t][at_block(i, STRIP), :]

    total[...] = jnp.zeros(total.shape, F32)

    @pl.loop(0, width // BLOCK)
    def _(i):
        total[...] += jnp.dot(
            rows_ref[:, at_block(step * (width // BLOCK) + i, BLOCK)],
            weight[at_block(i, BLOCK), :],
            preferred_element_type=F32,
        )

    values[...] = total[...].astype(BF16)

    @pl.loop(0, heads)
    def _(h):
        out = jnp.dot(
            attn_ref[step, at_block(begin + h, lat), :], values[...], preferred_element_type=F32
        )
        part = (out - target_ref[...]) * 0.0625
        resid[at_block(h, lat), :] = of_head(h, head_size, part).astype(BF16)

    @pl.loop(0, win // BLOCK)
    def _(j):
        dvalues[at_block(j, BLOCK), :] = lax.dot_general(
            attn_ref[step, at_block(begin // heads, heads * lat), at_block(j, BLOCK)],
            resid[...],
            (((0,), (0,)), ((), ())),
            preferred_element_type=F32,
        ).astype(BF16)

    @pl.loop(0, width // BLOCK)
    def _(i):
        at = at_block(i, BLOCK)
        new = jnp.dot(turned_ref[step, at, :], dvalues[...], preferred_element_type=F32)
        if last:
            grad_ref, track_ref = extra
            new = 0.5 * track_ref[0, at, :] + new - grad_ref[0, at, :]
        out_ref[0, at, :] = new


def gradient(chain, rows, turned, attn, targets, step, starts, group, weights, extra=()):
    lat, width = targets.shape
    win = rows.shape[0]
    head_size = width // HEADS
    span = weights[0].shape[1]
    first = starts[0] // group
    each = pl.BlockSpec((1, width, span), lambda t: (t, 0, 0))
    ins = [
        (rows, WHOLE),
        (turned, WHOLE),
        (attn, WHOLE),
        (targets, pl.BlockSpec((lat, span), lambda t: (0, first + t))),
    ]
    ins += [(a, WHOLE) for a in weights] + [(a, each) for a in extra]
    return chain.call(
        partial(
            grad_body, step=step, starts=starts, heads=group, head_size=head_size, last=bool(extra)
        ),
        "gradient",
        (len(starts),),
        ins,
        [(shape((len(starts), width, span), F32), each)],
        vmem=20,
        scratch=[
            pltpu.VMEM((width, span), BF16),
            pltpu.VMEM((win, span), F32),
            pltpu.VMEM((win, span), BF16),
            pltpu.VMEM((group * lat, span), BF16),
            pltpu.VMEM((win, span), BF16),
        ],
    )[0]


def mix_body(*refs):
    def strip(weight_ref, track_ref, got_ref, new_ref, sent_ref):
        new = 0.5 * (weight_ref[...] + got_ref[...].astype(F32)) - 0.05 * track_ref[...]
        new_ref[...] = new
        sent_ref[...] = new.astype(BF16)

    in_strips(strip, *refs)


def mix_weight(chain, weight, track, got, at, block_rows=256):
    rows, span = got.shape
    wide = pl.BlockSpec((block_rows, span), lambda i: (i, at))
    own = pl.BlockSpec((block_rows, span), lambda i: (i, 0))
    return chain.call(
        mix_body,
        "mix_weight",
        (rows // block_rows,),
        [(weight, wide), (track, wide), (got, own)],
        [(shape((rows, span), F32), own), (shape((rows, span), BF16), own)],
        vmem=8,
    )


def update_body(*refs):
    def strip(track, track_got, grad, old, weight, weight_got, track_out, track_sent, weight_out, weight_used):
        new_track = 0.5 * (track[...] + track_got[...].astype(F32)) + grad[...] - old[...]
        track_out[...] = new_track
        track_sent[...] = new_track.astype(BF16)
        new_weight = 0.5 * (weight[...] + weight_got[...].astype(F32)) - 0.05 * new_track
        weight_out[...] = new_weight
        weight_used[...] = new_weight.astype(BF16)

    in_strips(strip, *refs[:6], *refs[-4:])


def update(chain, trackers, track_got, grad, old, weight, weight_got, wholes, at, part, block_rows=256):
    rows, span = weight.shape
    width = trackers.shape[1]
    wide = pl.BlockSpec((block_rows, span), lambda i: (i, at))
    own = pl.BlockSpec((block_rows, span), lambda i: (i, 0))
    mine = pl.BlockSpec((1, block_rows, span), lambda i: (part, i, 0))
    ins = [
        (trackers, wide),
        (track_got, own),
        (grad, mine),
        (old, wide),
        (weight, own),
        (weight_got, own),
    ]
    aliases = {}
    for out, whole in zip((0, 2), wholes):
        if whole is not None:
            aliases[len(ins)] = out
            ins.append((whole, pl.BlockSpec(memory_space=pl.ANY)))
    return chain.call(
        update_body,
        "update",
        (rows // block_rows,),
        ins,
        [
            (shape(grad.shape, F32), mine),
            (shape((rows, span), BF16), own),
            (pltpu.HBM((rows, width), F32), wide),
            (shape((rows, span), BF16), own),
        ],
        vmem=12,
        aliases=aliases,
    )


def place_body(*refs):
    def strip(part_ref, got_ref, out_ref):
        out_ref[...] = part_ref[...] + 0.5 * got_ref[...].astype(F32)

    in_strips(strip, *refs[:2], refs[-1])


def place(chain, part, got, whole, at, number, width, block_rows=256):
    rows, span = got.shape
    own = pl.BlockSpec((block_rows, span), lambda i: (i, 0))
    ins = [(part, pl.BlockSpec((1, block_rows, span), lambda i: (number, i, 0))), (got, own)]
    if whole is not None:
        ins.append((whole, pl.BlockSpec(memory_space=pl.ANY)))
    return chain.call(
        place_body,
        "place",
        (rows // block_rows,),
        ins,
        [(pltpu.HBM((rows, width), F32), pl.BlockSpec((block_rows, span), lambda i: (i, at)))],
        vmem=8,
        aliases={} if whole is None else {2: 0},
    )[0]


def from_partner(value, bit):
    size = lax.axis_size("dp")
    return lax.ppermute(value, "dp", [(s, s ^ (1 << bit)) for s in range(size)])


def exchange_rows(packed, count_dev):
    slots, width = packed.shape
    blocks = packed.reshape(count_dev, slots // count_dev, width)
    got = lax.all_to_all(blocks, "dp", split_axis=0, concat_axis=0, tiled=True)
    return got.reshape(slots, width)


def plan(bits, count):
    on_chip = bits[0] == 0
    half = count // 2
    order = [("pack", 0), ("send", 0), ("send", 1), ("send", 2)]
    for c in range(count):
        if c == half and not on_chip:
            order += [("attn", 0)]
        order += [("hold_x", c - 2), ("mix", c), ("send", c + 3)]
        if c == half and not on_chip:
            order += [("grad", 0)]
    order += [("hold_x", count - 2)]
    order += [("attn", 0), ("grad", 0)] if on_chip else [("grad", 1)]
    for c in range(count):
        if c == half and on_chip:
            order += [("grad", 1)]
        if c == (half if on_chip else 0):
            order += [("hold_x", count - 1)]
        order += [("hold_y", c - 2), ("update", c), ("send", count + 3 + c)]
        if c == half - 1 and not on_chip:
            order += [("final", 0)]
    if on_chip:
        order += [("final", 0)]
    return order + [("place", 0), ("final", 1)] + [("place", c) for c in range(1, count)]


def two_steps(dest, tokens, params, trackers, old_grads, key_weight, latents, targets, *, bits):
    count_dev = lax.axis_size("dp")
    width = params.shape[1]
    head_size = width // HEADS
    count = len(GROUPS)
    half = count // 2
    spans = [g * head_size for g in GROUPS]
    starts = [sum(GROUPS[:c]) for c in range(count)]
    at = [s // g for s, g in zip(starts, GROUPS)]
    first, second = bits

    chain = Chain()
    got0, x1, x1b, x1_got, x2b, y1_got = {}, {}, {}, {}, {}, {}
    g1, y1, part = [None, None], [None, None], [None, None]
    rows = attn = turned = new_params = new_trackers = None
    for what, c in plan(bits, count):
        if what == "pack":
            rows = exchange_rows(pack_rows(chain, dest, tokens, count_dev), count_dev)
        elif what == "send" and c < 2 * count:
            whole, i = (params, c) if c < count else (trackers, c - count)
            got0[c] = from_partner(round_columns(chain, whole, at[i], spans[i]), first)
        elif what == "hold_x" and c >= 0:
            chain.hold(x1_got[c])
        elif what == "hold_y" and c >= 0:
            chain.hold(y1_got[c])
        elif what == "mix":
            x1[c], x1b[c] = mix_weight(chain, params, trackers, got0[c], at[c])
            x1_got[c] = from_partner(x1b[c], second)
        elif what == "attn":
            attn, turned = attention(chain, rows, key_weight, latents)
        elif what in ("grad", "final"):
            some = range(c * half, (c + 1) * half)
            last = what == "final"
            (part if last else g1)[c] = gradient(
                chain,
                rows,
                turned,
                attn,
                targets,
                1 if last else 0,
                [starts[i] for i in some],
                GROUPS[some[0]],
                [(x2b if last else x1b)[i] for i in some],
                (g1[c], y1[c]) if last else (),
            )
        elif what == "update":
            h = c // half
            y1[h], sent, new_params, x2b[c] = update(
                chain,
                trackers,
                got0[count + c],
                g1[h],
                old_grads,
                x1[c],
                x1_got[c],
                (y1[h], new_params),
                at[c],
                c % half,
            )
            y1_got[c] = from_partner(sent, second)
        elif what == "place":
            new_trackers = place(
                chain, part[c // half], y1_got[c], new_trackers, at[c], c % half, width
            )
    return new_params, new_trackers


def shards(step_index, dest, tokens, params, trackers, old_grads, key_weight, latents, targets):
    logn = lax.axis_size("dp").bit_length() - 1
    branches = [partial(two_steps, bits=(b, (b + 1) % logn)) for b in range(logn)]
    return lax.switch(
        lax.rem(step_index[0], logn),
        branches,
        dest[:, :, 0],
        tokens,
        params,
        trackers,
        old_grads,
        key_weight,
        latents,
        targets,
    )


def solution(mesh):
    in_specs = (
        P(),
        P(None, "dp", None),
        P(None, "dp", None),
        P("dp", None),
        P("dp", None),
        P("dp", None),
        P(),
        P(),
        P("dp", None),
    )
    out_specs = (P("dp", None), P("dp", None))
    return jax.shard_map(shards, mesh=mesh, in_specs=in_specs, out_specs=out_specs, check_vma=False)
```

```python
from functools import partial

import jax
import jax.numpy as jnp
from jax import lax
from jax.experimental import pallas as pl
from jax.experimental.pallas import tpu as pltpu
from jax.sharding import PartitionSpec as P

HEADS = 16
STEPS = 2
GROUPS = (4, 4, 4, 4)
ATTN_HEADS = 4
F32 = jnp.float32
BF16 = jnp.bfloat16


class Chain:
    def __init__(self):
        self.token = None
        self.held = []

    def hold(self, value):
        self.held.append(value)

    def call(self, body, name, grid, ins, outs, vmem, aliases=None, scratch=(), flops=1):
        after = self.held + ([] if self.token is None else [self.token])
        self.held = []
        arrays = [a for a, _ in ins] + after
        specs = [s for _, s in ins] + [pl.BlockSpec(memory_space=pl.ANY)] * len(after)
        count_in, count_out = len(ins), len(outs)

        def kernel(*refs):
            given_out = len(arrays) + count_out
            body(*refs[:count_in], *refs[len(arrays) : given_out], *refs[given_out + 1 :])

        given = pl.pallas_call(
            kernel,
            out_shape=tuple(o for o, _ in outs) + (jax.ShapeDtypeStruct((8, 128), F32),),
            grid=grid,
            scratch_shapes=list(scratch),
            in_specs=specs,
            out_specs=tuple(s for _, s in outs) + (pl.BlockSpec(memory_space=pl.ANY),),
            input_output_aliases=dict(aliases or {}),
            compiler_params=pltpu.CompilerParams(vmem_limit_bytes=vmem * 1024 * 1024),
            cost_estimate=pl.CostEstimate(flops=flops, bytes_accessed=1, transcendentals=0),
            name=name,
        )(*arrays)
        self.token = given[-1]
        return given[:-1]


BLOCK = 256
STRIP = 32
EARLY = 10**11


def at_block(i, size):
    return pl.ds(pl.multiple_of(i * size, size), size)


def in_strips(body, *refs):
    flat = [ref.at[0] if len(ref.shape) == 3 else ref for ref in refs]

    @pl.loop(0, flat[0].shape[0] // STRIP)
    def _(i):
        body(*[ref.at[at_block(i, STRIP), :] for ref in flat])


def shape(dims, dtype):
    return jax.ShapeDtypeStruct(dims, dtype)


def pack_body(dest_ref, tokens_ref, out_ref, *, count_dev, cap):
    owner = dest_ref[0]
    rows = owner.shape[1]
    trainer = lax.broadcasted_iota(jnp.int32, (count_dev, rows), 0)
    named = (trainer == owner).astype(F32)
    earlier = lax.broadcasted_iota(jnp.int32, (rows, rows), 0) < lax.broadcasted_iota(
        jnp.int32, (rows, rows), 1
    )
    before = jnp.dot(
        named.astype(BF16), earlier.astype(F32).astype(BF16), preferred_element_type=F32
    )
    rank = jnp.sum(named * before, axis=0, keepdims=True).astype(jnp.int32)
    where = owner * cap + rank

    @pl.loop(0, out_ref.shape[0] // BLOCK)
    def _(i):
        slot = lax.broadcasted_iota(jnp.int32, (BLOCK, rows), 0) + i * BLOCK
        chosen = (slot == where).astype(F32).astype(BF16)
        out_ref[at_block(i, BLOCK), :] = jnp.dot(
            chosen, tokens_ref[0], preferred_element_type=F32
        ).astype(BF16)


def pack_rows(chain, dest, tokens, count_dev):
    steps, rows, width = tokens.shape
    cap = 2 * rows // count_dev
    slots = count_dev * cap
    span = width
    return chain.call(
        partial(pack_body, count_dev=count_dev, cap=cap),
        "pack_rows",
        (steps, width // span),
        [
            (dest.reshape(steps, 1, rows), pl.BlockSpec((1, 1, rows), lambda k, i: (k, 0, 0))),
            (tokens, pl.BlockSpec((1, rows, span), lambda k, i: (k, 0, i))),
        ],
        [
            (
                shape((slots, steps * width), BF16),
                pl.BlockSpec((slots, span), lambda k, i: (0, k * (width // span) + i)),
            )
        ],
        vmem=16,
    )[0]


def round_body(*refs):
    def strip(src_ref, out_ref):
        out_ref[...] = src_ref[...].astype(BF16)

    in_strips(strip, *refs)


def round_columns(chain, whole, at, span, block_rows=256):
    rows = whole.shape[0]
    return chain.call(
        round_body,
        "round_columns",
        (rows // block_rows,),
        [(whole, pl.BlockSpec((block_rows, span), lambda i: (i, at)))],
        [(shape((rows, span), BF16), pl.BlockSpec((block_rows, span), lambda i: (i, 0)))],
        vmem=4,
    )[0]


def of_head(head, head_size, value):
    column = lax.broadcasted_iota(jnp.int32, value.shape, 1) // head_size
    return jnp.where(column == head, value, 0.0)


def attn_body(rows_ref, key_ref, lat_ref, attn_ref, turned_ref, *, heads, head_size):
    @pl.when(pl.program_id(1) == 0)
    def _():
        @pl.loop(0, rows_ref.shape[0] // BLOCK)
        def _(j):
            turned_ref[0, :, at_block(j, BLOCK)] = rows_ref[at_block(j, BLOCK), :].T

    latents = lat_ref[...].astype(F32)
    queries = jnp.concatenate(
        [of_head(h, head_size, latents).astype(BF16) for h in range(heads)], axis=0
    )

    @pl.loop(0, rows_ref.shape[0] // BLOCK)
    def _(j):
        keys = jnp.dot(
            rows_ref[at_block(j, BLOCK), :], key_ref[...], preferred_element_type=F32
        ).astype(BF16)
        scores = lax.dot_general(
            queries, keys, (((1,), (1,)), ((), ())), preferred_element_type=F32
        )
        scores = scores * (1.0 / head_size**0.5) - 3.5
        attn_ref[0, :, at_block(j, BLOCK)] = jax.nn.sigmoid(scores).astype(BF16)


WHOLE = pl.BlockSpec(memory_space=pltpu.VMEM)


def attention(chain, rows, key_weight, latents):
    win = rows.shape[0]
    lat, width = latents.shape
    head_size = width // HEADS
    span = ATTN_HEADS * head_size
    return chain.call(
        partial(attn_body, heads=ATTN_HEADS, head_size=head_size),
        "attention",
        (STEPS, HEADS // ATTN_HEADS),
        [
            (rows, pl.BlockSpec((win, width), lambda k, c: (0, k))),
            (key_weight, pl.BlockSpec((width, span), lambda k, c: (0, c))),
            (latents, pl.BlockSpec((lat, span), lambda k, c: (0, c))),
        ],
        [
            (
                shape((STEPS, HEADS * lat, win), BF16),
                pl.BlockSpec((1, ATTN_HEADS * lat, win), lambda k, c: (k, c, 0)),
            ),
            (
                shape((STEPS, width, win), BF16),
                pl.BlockSpec((1, width, win), lambda k, c: (k, 0, 0)),
            ),
        ],
        vmem=16,
    )


def grad_body(*refs, step, starts, heads, head_size, last):
    count = len(starts)
    rows_ref, turned_ref, attn_ref, target_ref = refs[:4]
    weight_refs = refs[4 : 4 + count]
    extra = refs[4 + count : -6]
    out_ref, weight, total, values, resid, dvalues = refs[-6:]
    win, span = values.shape
    lat = resid.shape[0] // heads
    width = weight.shape[0]
    now = pl.program_id(0)
    begin = starts[0] + now * heads

    for t in range(count):

        @pl.when(now == t)
        def _(t=t):
            @pl.loop(0, width // STRIP)
            def _(i):
                weight[at_block(i, STRIP), :] = weight_refs[t][at_block(i, STRIP), :]

    total[...] = jnp.zeros(total.shape, F32)

    @pl.loop(0, width // BLOCK)
    def _(i):
        total[...] += jnp.dot(
            rows_ref[:, at_block(step * (width // BLOCK) + i, BLOCK)],
            weight[at_block(i, BLOCK), :],
            preferred_element_type=F32,
        )

    values[...] = total[...].astype(BF16)

    @pl.loop(0, heads)
    def _(h):
        out = jnp.dot(
            attn_ref[step, at_block(begin + h, lat), :], values[...], preferred_element_type=F32
        )
        part = (out - target_ref[...]) * 0.0625
        resid[at_block(h, lat), :] = of_head(h, head_size, part).astype(BF16)

    @pl.loop(0, win // BLOCK)
    def _(j):
        dvalues[at_block(j, BLOCK), :] = lax.dot_general(
            attn_ref[step, at_block(begin // heads, heads * lat), at_block(j, BLOCK)],
            resid[...],
            (((0,), (0,)), ((), ())),
            preferred_element_type=F32,
        ).astype(BF16)

    @pl.loop(0, width // BLOCK)
    def _(i):
        at = at_block(i, BLOCK)
        new = jnp.dot(turned_ref[step, at, :], dvalues[...], preferred_element_type=F32)
        if last:
            grad_ref, track_ref = extra
            new = 0.5 * track_ref[0, at, :] + new - grad_ref[0, at, :]
        out_ref[0, at, :] = new


def gradient(chain, rows, turned, attn, targets, step, starts, group, weights, extra=()):
    lat, width = targets.shape
    win = rows.shape[0]
    head_size = width // HEADS
    span = weights[0].shape[1]
    first = starts[0] // group
    each = pl.BlockSpec((1, width, span), lambda t: (t, 0, 0))
    ins = [
        (rows, WHOLE),
        (turned, WHOLE),
        (attn, WHOLE),
        (targets, pl.BlockSpec((lat, span), lambda t: (0, first + t))),
    ]
    ins += [(a, WHOLE) for a in weights] + [(a, each) for a in extra]
    return chain.call(
        partial(
            grad_body, step=step, starts=starts, heads=group, head_size=head_size, last=bool(extra)
        ),
        "gradient",
        (len(starts),),
        ins,
        [(shape((len(starts), width, span), F32), each)],
        vmem=20,
        scratch=[
            pltpu.VMEM((width, span), BF16),
            pltpu.VMEM((win, span), F32),
            pltpu.VMEM((win, span), BF16),
            pltpu.VMEM((group * lat, span), BF16),
            pltpu.VMEM((win, span), BF16),
        ],
    )[0]


def mix_body(*refs):
    def strip(weight_ref, track_ref, got_ref, new_ref, sent_ref):
        new = 0.5 * (weight_ref[...] + got_ref[...].astype(F32)) - 0.05 * track_ref[...]
        new_ref[...] = new
        sent_ref[...] = new.astype(BF16)

    in_strips(strip, *refs)


def mix_weight(chain, weight, track, got, at, flops, block_rows=256):
    rows, span = got.shape
    wide = pl.BlockSpec((block_rows, span), lambda i: (i, at))
    own = pl.BlockSpec((block_rows, span), lambda i: (i, 0))
    return chain.call(
        mix_body,
        "mix_weight",
        (rows // block_rows,),
        [(weight, wide), (track, wide), (got, own)],
        [(shape((rows, span), F32), own), (shape((rows, span), BF16), own)],
        vmem=8,
        flops=flops,
    )


def update_body(*refs):
    def strip(track, track_got, grad, old, weight, weight_got, track_out, track_sent, weight_out, weight_used):
        new_track = 0.5 * (track[...] + track_got[...].astype(F32)) + grad[...] - old[...]
        track_out[...] = new_track
        track_sent[...] = new_track.astype(BF16)
        new_weight = 0.5 * (weight[...] + weight_got[...].astype(F32)) - 0.05 * new_track
        weight_out[...] = new_weight
        weight_used[...] = new_weight.astype(BF16)

    in_strips(strip, *refs[:6], *refs[-4:])


def update(chain, trackers, track_got, grad, old, weight, weight_got, wholes, at, part, block_rows=256):
    rows, span = weight.shape
    width = trackers.shape[1]
    wide = pl.BlockSpec((block_rows, span), lambda i: (i, at))
    own = pl.BlockSpec((block_rows, span), lambda i: (i, 0))
    mine = pl.BlockSpec((1, block_rows, span), lambda i: (part, i, 0))
    ins = [
        (trackers, wide),
        (track_got, own),
        (grad, mine),
        (old, wide),
        (weight, own),
        (weight_got, own),
    ]
    aliases = {}
    for out, whole in zip((0, 2), wholes):
        if whole is not None:
            aliases[len(ins)] = out
            ins.append((whole, pl.BlockSpec(memory_space=pl.ANY)))
    return chain.call(
        update_body,
        "update",
        (rows // block_rows,),
        ins,
        [
            (shape(grad.shape, F32), mine),
            (shape((rows, span), BF16), own),
            (pltpu.HBM((rows, width), F32), wide),
            (shape((rows, span), BF16), own),
        ],
        vmem=12,
        aliases=aliases,
    )


def place_body(*refs):
    def strip(part_ref, got_ref, out_ref):
        out_ref[...] = part_ref[...] + 0.5 * got_ref[...].astype(F32)

    in_strips(strip, *refs[:2], refs[-1])


def place(chain, part, got, whole, at, number, width, block_rows=256):
    rows, span = got.shape
    own = pl.BlockSpec((block_rows, span), lambda i: (i, 0))
    ins = [(part, pl.BlockSpec((1, block_rows, span), lambda i: (number, i, 0))), (got, own)]
    if whole is not None:
        ins.append((whole, pl.BlockSpec(memory_space=pl.ANY)))
    return chain.call(
        place_body,
        "place",
        (rows // block_rows,),
        ins,
        [(pltpu.HBM((rows, width), F32), pl.BlockSpec((block_rows, span), lambda i: (i, at)))],
        vmem=8,
        aliases={} if whole is None else {2: 0},
    )[0]


def from_partner(value, bit):
    size = lax.axis_size("dp")
    return lax.ppermute(value, "dp", [(s, s ^ (1 << bit)) for s in range(size)])


def exchange_rows(packed, count_dev):
    slots, width = packed.shape
    blocks = packed.reshape(count_dev, slots // count_dev, width)
    got = lax.all_to_all(blocks, "dp", split_axis=0, concat_axis=0, tiled=True)
    return got.reshape(slots, width)


def plan(bits, count):
    half = count // 2
    order = [("send", 0), ("send", 1), ("pack", 0), ("send", 2)]
    if bits[0] == 0:
        for c in range(count):
            order += [("hold_x", c - 2), ("mix", c), ("send", c + 3)]
        order += [("attn", 0), ("hold_x", count - 2), ("grad", 0)]
        for c in range(count):
            if c == half:
                order += [("grad", 1), ("hold_x", count - 1)]
            order += [("hold_y", c - 2), ("update", c), ("send", count + 3 + c)]
        order += [("final", 0), ("place", 0), ("final", 1)]
        return order + [("place", c) for c in range(1, count)]
    for c in range(count):
        order += [("hold_x", c - 2), ("mix", c), ("send", c + 3)]
        if c == half:
            order += [("attn", 0)]
    order += [("hold_x", count - 2), ("grad", 0)]
    done = 0
    for c in range(count):
        if c == half:
            order += [("grad", 1), ("hold_x", count - 1)]
        order += [("hold_y", c - 2), ("update", c), ("send", count + 3 + c)]
        if c == (half - 1 if max(bits) > 3 else half):
            order += [("final", 0)]
        if c >= half and max(bits) > 3:
            order += [("place", done)]
            done += 1
    order += [] if done else [("place", 0)]
    order += [("final", 1)]
    return order + [("place", c) for c in range(max(done, 1), count)]


def two_steps(dest, tokens, params, trackers, old_grads, key_weight, latents, targets, *, bits):
    count_dev = lax.axis_size("dp")
    width = params.shape[1]
    head_size = width // HEADS
    count = len(GROUPS)
    half = count // 2
    spans = [g * head_size for g in GROUPS]
    starts = [sum(GROUPS[:c]) for c in range(count)]
    at = [s // g for s, g in zip(starts, GROUPS)]
    first, second = bits

    chain = Chain()
    got0, x1, x1b, x1_got, x2b, y1_got = {}, {}, {}, {}, {}, {}
    g1, y1, part = [None, None], [None, None], [None, None]
    rows = attn = turned = new_params = new_trackers = None
    for what, c in plan(bits, count):
        if what == "pack":
            rows = exchange_rows(pack_rows(chain, dest, tokens, count_dev), count_dev)
        elif what == "send" and c < 2 * count:
            whole, i = (params, c) if c < count else (trackers, c - count)
            got0[c] = from_partner(round_columns(chain, whole, at[i], spans[i]), first)
        elif what == "hold_x" and c >= 0:
            chain.hold(x1_got[c])
        elif what == "hold_y" and c >= 0:
            chain.hold(y1_got[c])
        elif what == "mix":
            x1[c], x1b[c] = mix_weight(
                chain, params, trackers, got0[c], at[c], EARLY if c == 0 else 1
            )
            x1_got[c] = from_partner(x1b[c], second)
        elif what == "attn":
            attn, turned = attention(chain, rows, key_weight, latents)
        elif what in ("grad", "final"):
            some = range(c * half, (c + 1) * half)
            last = what == "final"
            (part if last else g1)[c] = gradient(
                chain,
                rows,
                turned,
                attn,
                targets,
                1 if last else 0,
                [starts[i] for i in some],
                GROUPS[some[0]],
                [(x2b if last else x1b)[i] for i in some],
                (g1[c], y1[c]) if last else (),
            )
        elif what == "update":
            h = c // half
            y1[h], sent, new_params, x2b[c] = update(
                chain,
                trackers,
                got0[count + c],
                g1[h],
                old_grads,
                x1[c],
                x1_got[c],
                (y1[h], new_params),
                at[c],
                c % half,
            )
            y1_got[c] = from_partner(sent, second)
        elif what == "place":
            new_trackers = place(
                chain, part[c // half], y1_got[c], new_trackers, at[c], c % half, width
            )
    return new_params, new_trackers


def shards(step_index, dest, tokens, params, trackers, old_grads, key_weight, latents, targets):
    logn = lax.axis_size("dp").bit_length() - 1
    branches = [partial(two_steps, bits=(b, (b + 1) % logn)) for b in range(logn)]
    return lax.switch(
        lax.rem(step_index[0], logn),
        branches,
        dest[:, :, 0],
        tokens,
        params,
        trackers,
        old_grads,
        key_weight,
        latents,
        targets,
    )


def solution(mesh):
    in_specs = (
        P(),
        P(None, "dp", None),
        P(None, "dp", None),
        P("dp", None),
        P("dp", None),
        P("dp", None),
        P(),
        P(),
        P("dp", None),
    )
    out_specs = (P("dp", None), P("dp", None))
    return jax.shard_map(shards, mesh=mesh, in_specs=in_specs, out_specs=out_specs, check_vma=False)
```

```python
from functools import partial

import jax
import jax.numpy as jnp
from jax import lax
from jax.experimental import pallas as pl
from jax.experimental.pallas import tpu as pltpu
from jax.sharding import PartitionSpec as P

HEADS = 16
STEPS = 2
GROUPS = (4, 4, 4, 4)
ATTN_HEADS = 4
F32 = jnp.float32
BF16 = jnp.bfloat16


class Chain:
    def __init__(self):
        self.token = None
        self.held = []

    def hold(self, value):
        self.held.append(value)

    def call(self, body, name, grid, ins, outs, vmem, aliases=None, scratch=(), flops=1):
        after = self.held + ([] if self.token is None else [self.token])
        self.held = []
        arrays = [a for a, _ in ins] + after
        specs = [s for _, s in ins] + [pl.BlockSpec(memory_space=pl.ANY)] * len(after)
        count_in, count_out = len(ins), len(outs)

        def kernel(*refs):
            given_out = len(arrays) + count_out
            body(*refs[:count_in], *refs[len(arrays) : given_out], *refs[given_out + 1 :])

        given = pl.pallas_call(
            kernel,
            out_shape=tuple(o for o, _ in outs) + (jax.ShapeDtypeStruct((8, 128), F32),),
            grid=grid,
            scratch_shapes=list(scratch),
            in_specs=specs,
            out_specs=tuple(s for _, s in outs) + (pl.BlockSpec(memory_space=pl.ANY),),
            input_output_aliases=dict(aliases or {}),
            compiler_params=pltpu.CompilerParams(vmem_limit_bytes=vmem * 1024 * 1024),
            cost_estimate=pl.CostEstimate(flops=flops, bytes_accessed=1, transcendentals=0),
            name=name,
        )(*arrays)
        self.token = given[-1]
        return given[:-1]


BLOCK = 256
STRIP = 32
EARLY = 10**11


def at_block(i, size):
    return pl.ds(pl.multiple_of(i * size, size), size)


def in_strips(body, *refs):
    flat = [ref.at[0] if len(ref.shape) == 3 else ref for ref in refs]

    @pl.loop(0, flat[0].shape[0] // STRIP)
    def _(i):
        body(*[ref.at[at_block(i, STRIP), :] for ref in flat])


def shape(dims, dtype):
    return jax.ShapeDtypeStruct(dims, dtype)


def pack_body(dest_ref, tokens_ref, out_ref, *, count_dev, cap):
    owner = dest_ref[0]
    rows = owner.shape[1]
    trainer = lax.broadcasted_iota(jnp.int32, (count_dev, rows), 0)
    named = (trainer == owner).astype(F32)
    earlier = lax.broadcasted_iota(jnp.int32, (rows, rows), 0) < lax.broadcasted_iota(
        jnp.int32, (rows, rows), 1
    )
    before = jnp.dot(
        named.astype(BF16), earlier.astype(F32).astype(BF16), preferred_element_type=F32
    )
    rank = jnp.sum(named * before, axis=0, keepdims=True).astype(jnp.int32)
    where = owner * cap + rank

    @pl.loop(0, out_ref.shape[0] // BLOCK)
    def _(i):
        slot = lax.broadcasted_iota(jnp.int32, (BLOCK, rows), 0) + i * BLOCK
        chosen = (slot == where).astype(F32).astype(BF16)
        out_ref[at_block(i, BLOCK), :] = jnp.dot(
            chosen, tokens_ref[0], preferred_element_type=F32
        ).astype(BF16)


def pack_rows(chain, dest, tokens, count_dev):
    steps, rows, width = tokens.shape
    cap = 2 * rows // count_dev
    slots = count_dev * cap
    span = width
    return chain.call(
        partial(pack_body, count_dev=count_dev, cap=cap),
        "pack_rows",
        (steps, width // span),
        [
            (dest.reshape(steps, 1, rows), pl.BlockSpec((1, 1, rows), lambda k, i: (k, 0, 0))),
            (tokens, pl.BlockSpec((1, rows, span), lambda k, i: (k, 0, i))),
        ],
        [
            (
                shape((slots, steps * width), BF16),
                pl.BlockSpec((slots, span), lambda k, i: (0, k * (width // span) + i)),
            )
        ],
        vmem=16,
    )[0]


def round_body(*refs):
    def strip(src_ref, out_ref):
        out_ref[...] = src_ref[...].astype(BF16)

    in_strips(strip, *refs)


def round_columns(chain, whole, at, span, block_rows=256):
    rows = whole.shape[0]
    return chain.call(
        round_body,
        "round_columns",
        (rows // block_rows,),
        [(whole, pl.BlockSpec((block_rows, span), lambda i: (i, at)))],
        [(shape((rows, span), BF16), pl.BlockSpec((block_rows, span), lambda i: (i, 0)))],
        vmem=4,
    )[0]


def of_head(head, head_size, value):
    column = lax.broadcasted_iota(jnp.int32, value.shape, 1) // head_size
    return jnp.where(column == head, value, 0.0)


def attn_body(rows_ref, key_ref, lat_ref, attn_ref, turned_ref, *, heads, head_size):
    @pl.when(pl.program_id(1) == 0)
    def _():
        @pl.loop(0, rows_ref.shape[0] // BLOCK)
        def _(j):
            turned_ref[0, :, at_block(j, BLOCK)] = rows_ref[at_block(j, BLOCK), :].T

    latents = lat_ref[...].astype(F32)
    queries = jnp.concatenate(
        [of_head(h, head_size, latents).astype(BF16) for h in range(heads)], axis=0
    )

    @pl.loop(0, rows_ref.shape[0] // BLOCK)
    def _(j):
        keys = jnp.dot(
            rows_ref[at_block(j, BLOCK), :], key_ref[...], preferred_element_type=F32
        ).astype(BF16)
        scores = lax.dot_general(
            queries, keys, (((1,), (1,)), ((), ())), preferred_element_type=F32
        )
        scores = scores * (1.0 / head_size**0.5) - 3.5
        attn_ref[0, :, at_block(j, BLOCK)] = jax.nn.sigmoid(scores).astype(BF16)


WHOLE = pl.BlockSpec(memory_space=pltpu.VMEM)


def attention(chain, rows, key_weight, latents):
    win = rows.shape[0]
    lat, width = latents.shape
    head_size = width // HEADS
    span = ATTN_HEADS * head_size
    return chain.call(
        partial(attn_body, heads=ATTN_HEADS, head_size=head_size),
        "attention",
        (STEPS, HEADS // ATTN_HEADS),
        [
            (rows, pl.BlockSpec((win, width), lambda k, c: (0, k))),
            (key_weight, pl.BlockSpec((width, span), lambda k, c: (0, c))),
            (latents, pl.BlockSpec((lat, span), lambda k, c: (0, c))),
        ],
        [
            (
                shape((STEPS, HEADS * lat, win), BF16),
                pl.BlockSpec((1, ATTN_HEADS * lat, win), lambda k, c: (k, c, 0)),
            ),
            (
                shape((STEPS, width, win), BF16),
                pl.BlockSpec((1, width, win), lambda k, c: (k, 0, 0)),
            ),
        ],
        vmem=16,
    )


def grad_body(*refs, step, starts, heads, head_size, last):
    count = len(starts)
    rows_ref, turned_ref, attn_ref, target_ref = refs[:4]
    weight_refs = refs[4 : 4 + count]
    extra = refs[4 + count : -4]
    out_ref, weight, resid, dvalues = refs[-4:]
    lat = resid.shape[0] // heads
    width = weight.shape[0]
    now = pl.program_id(0)
    begin = starts[0] + now * heads

    for t in range(count):

        @pl.when(now == t)
        def _(t=t):
            @pl.loop(0, width // STRIP)
            def _(i):
                weight[at_block(i, STRIP), :] = weight_refs[t][at_block(i, STRIP), :]

    values = jnp.dot(
        rows_ref[:, pl.ds(step * width, width)], weight[...], preferred_element_type=F32
    ).astype(BF16)
    attn = attn_ref[step, at_block(begin // heads, heads * lat), :]
    out = jnp.dot(attn, values, preferred_element_type=F32)
    target = target_ref[...]
    for h in range(heads):
        part = (out[h * lat : (h + 1) * lat, :] - target) * 0.0625
        resid[h * lat : (h + 1) * lat, :] = of_head(h, head_size, part).astype(BF16)
    dvalues[...] = lax.dot_general(
        attn, resid[...], (((0,), (0,)), ((), ())), preferred_element_type=F32
    ).astype(BF16)

    @pl.loop(0, width // BLOCK)
    def _(i):
        at = at_block(i, BLOCK)
        new = jnp.dot(turned_ref[step, at, :], dvalues[...], preferred_element_type=F32)
        if last:
            grad_ref, track_ref = extra[:2]
            new = 0.5 * track_ref[0, at, :] + new - grad_ref[0, at, :]
        out_ref[0, at, :] = new


def gradient(chain, rows, turned, attn, targets, step, some, weights, whole, extra=()):
    lat, width = targets.shape
    head_size = width // HEADS
    span = weights[0].shape[1]
    group = span // head_size
    first = some[0]
    each = pl.BlockSpec((1, width, span), lambda t: (first + t, 0, 0))
    ins = [
        (rows, WHOLE),
        (turned, WHOLE),
        (attn, WHOLE),
        (targets, pl.BlockSpec((lat, span), lambda t: (0, first + t))),
    ]
    ins += [(a, WHOLE) for a in weights] + [(a, each) for a in extra]
    aliases = {}
    if whole is not None:
        aliases = {len(ins): 0}
        ins.append((whole, pl.BlockSpec(memory_space=pl.ANY)))
    return chain.call(
        partial(
            grad_body,
            step=step,
            starts=[group * i for i in some],
            heads=group,
            head_size=head_size,
            last=bool(extra),
        ),
        "gradient",
        (len(some),),
        ins,
        [(shape((HEADS // group, width, span), F32), each)],
        vmem=20,
        aliases=aliases,
        scratch=[
            pltpu.VMEM((width, span), BF16),
            pltpu.VMEM((group * lat, span), BF16),
            pltpu.VMEM((rows.shape[0], span), BF16),
        ],
    )[0]


def mix_body(*refs):
    def strip(weight_ref, track_ref, got_ref, new_ref, sent_ref):
        new = 0.5 * (weight_ref[...] + got_ref[...].astype(F32)) - 0.05 * track_ref[...]
        new_ref[...] = new
        sent_ref[...] = new.astype(BF16)

    in_strips(strip, *refs)


def mix_weight(chain, weight, track, got, at, flops, block_rows=256):
    rows, span = got.shape
    wide = pl.BlockSpec((block_rows, span), lambda i: (i, at))
    own = pl.BlockSpec((block_rows, span), lambda i: (i, 0))
    return chain.call(
        mix_body,
        "mix_weight",
        (rows // block_rows,),
        [(weight, wide), (track, wide), (got, own)],
        [(shape((rows, span), F32), own), (shape((rows, span), BF16), own)],
        vmem=8,
        flops=flops,
    )


def update_body(*refs):
    def strip(track, track_got, grad, old, weight, weight_got, track_out, track_sent, weight_out, weight_used):
        new_track = 0.5 * (track[...] + track_got[...].astype(F32)) + grad[...] - old[...]
        track_out[...] = new_track
        track_sent[...] = new_track.astype(BF16)
        new_weight = 0.5 * (weight[...] + weight_got[...].astype(F32)) - 0.05 * new_track
        weight_out[...] = new_weight
        weight_used[...] = new_weight.astype(BF16)

    in_strips(strip, *refs[:6], *refs[-4:])


def update(chain, trackers, track_got, grad, old, weight, weight_got, wholes, at, part, block_rows=256):
    rows, span = weight.shape
    width = trackers.shape[1]
    wide = pl.BlockSpec((block_rows, span), lambda i: (i, at))
    own = pl.BlockSpec((block_rows, span), lambda i: (i, 0))
    mine = pl.BlockSpec((1, block_rows, span), lambda i: (part, i, 0))
    ins = [
        (trackers, wide),
        (track_got, own),
        (grad, mine),
        (old, wide),
        (weight, own),
        (weight_got, own),
    ]
    aliases = {}
    for out, whole in zip((0, 2), wholes):
        if whole is not None:
            aliases[len(ins)] = out
            ins.append((whole, pl.BlockSpec(memory_space=pl.ANY)))
    return chain.call(
        update_body,
        "update",
        (rows // block_rows,),
        ins,
        [
            (shape(grad.shape, F32), mine),
            (shape((rows, span), BF16), own),
            (pltpu.HBM((rows, width), F32), wide),
            (shape((rows, span), BF16), own),
        ],
        vmem=12,
        aliases=aliases,
    )


def place_body(*refs, count):
    part_ref, got_refs, out_ref = refs[0], refs[1 : 1 + count], refs[-1]
    span = got_refs[0].shape[1]

    @pl.loop(0, out_ref.shape[0] // STRIP)
    def _(i):
        at = at_block(i, STRIP)
        for t in range(count):
            out_ref[at, t * span : (t + 1) * span] = part_ref[t, at, :] + 0.5 * got_refs[t][
                at, :
            ].astype(F32)


def place(chain, part, gots, whole, first, width, block_rows=256):
    rows, span = gots[0].shape
    count = len(gots)
    own = pl.BlockSpec((block_rows, span), lambda i: (i, 0))
    ins = [(part, pl.BlockSpec((count, block_rows, span), lambda i: (first // count, i, 0)))]
    ins += [(got, own) for got in gots]
    aliases = {}
    if whole is not None:
        aliases = {len(ins): 0}
        ins.append((whole, pl.BlockSpec(memory_space=pl.ANY)))
    return chain.call(
        partial(place_body, count=count),
        "place",
        (rows // block_rows,),
        ins,
        [
            (
                pltpu.HBM((rows, width), F32),
                pl.BlockSpec((block_rows, count * span), lambda i: (i, first // count)),
            )
        ],
        vmem=12,
        aliases=aliases,
    )[0]


def from_partner(value, bit):
    size = lax.axis_size("dp")
    return lax.ppermute(value, "dp", [(s, s ^ (1 << bit)) for s in range(size)])


def exchange_rows(packed, count_dev):
    slots, width = packed.shape
    blocks = packed.reshape(count_dev, slots // count_dev, width)
    got = lax.all_to_all(blocks, "dp", split_axis=0, concat_axis=0, tiled=True)
    return got.reshape(slots, width)


def plan(bits, count):
    first, second = bits
    last = count - 1
    cut = count // 2
    if first == 0:
        order = [("pack", 0), ("send", 0), ("send", 1), ("send", 2)]
    else:
        order = [("send", 0), ("send", 1), ("pack", 0), ("send", 2)]
    for c in range(count):
        order += [("hold_x", c - 2), ("mix" if first == 0 or c else "mix_late", c), ("send", c + 3)]
        if c == count // 2 and first != 0:
            order += [("attn", 0)]
    order += [("attn", 0)] if first == 0 else []
    order += [("hold_x", count - 2), ("grad", 0)]
    for c in range(count):
        if c == cut:
            order += [("grad", 1), ("hold_x", last)]
        order += [("hold_y", c - 2), ("update", c), ("send", count + 3 + c)]
        if second == 0 and c == cut - 1:
            order += [("final", 0)]
        if second == 0 and c == cut:
            order += [("place", 0)]
    if second == 0:
        return cut, cut, order + [("final", 1), ("place", 1)]
    return cut, last, order + [("final", 2), ("place", 0), ("place", 1)]


def two_steps(dest, tokens, params, trackers, old_grads, key_weight, latents, targets, *, bits):
    count_dev = lax.axis_size("dp")
    width = params.shape[1]
    head_size = width // HEADS
    count = len(GROUPS)
    spans = [g * head_size for g in GROUPS]
    starts = [sum(GROUPS[:c]) for c in range(count)]
    at = [s // g for s, g in zip(starts, GROUPS)]
    first, second = bits

    chain = Chain()
    got0, x1, x1b, x1_got, x2b, y1_got = {}, {}, {}, {}, {}, {}
    rows = attn = turned = g1 = y1 = part = new_params = new_trackers = None
    cut, split, order = plan(bits, count)
    for what, c in order:
        if what == "pack":
            rows = exchange_rows(pack_rows(chain, dest, tokens, count_dev), count_dev)
        elif what == "send" and c < 2 * count:
            whole, i = (params, c) if c < count else (trackers, c - count)
            got0[c] = from_partner(round_columns(chain, whole, at[i], spans[i]), first)
        elif what == "hold_x" and c >= 0:
            chain.hold(x1_got[c])
        elif what == "hold_y" and c >= 0:
            chain.hold(y1_got[c])
        elif what in ("mix", "mix_late"):
            x1[c], x1b[c] = mix_weight(
                chain, params, trackers, got0[c], at[c], EARLY if what == "mix_late" else 1
            )
            x1_got[c] = from_partner(x1b[c], second)
        elif what == "attn":
            attn, turned = attention(chain, rows, key_weight, latents)
        elif what == "grad":
            some = range(cut, count) if c else range(cut)
            g1 = gradient(chain, rows, turned, attn, targets, 0, some, [x1b[i] for i in some], g1)
        elif what == "final":
            some = (range(cut), range(cut, count), range(count))[c]
            part = gradient(
                chain, rows, turned, attn, targets, 1, some, [x2b[i] for i in some], part, (g1, y1)
            )
        elif what == "update":
            y1, sent, new_params, x2b[c] = update(
                chain,
                trackers,
                got0[count + c],
                g1,
                old_grads,
                x1[c],
                x1_got[c],
                (y1, new_params),
                at[c],
                c,
            )
            y1_got[c] = from_partner(sent, second)
        elif what == "place":
            some = range(split, count) if c else range(split)
            new_trackers = place(
                chain, part, [y1_got[i] for i in some], new_trackers, some[0], width
            )
    return new_params, new_trackers


def shards(step_index, dest, tokens, params, trackers, old_grads, key_weight, latents, targets):
    logn = lax.axis_size("dp").bit_length() - 1
    branches = [partial(two_steps, bits=(b, (b + 1) % logn)) for b in range(logn)]
    return lax.switch(
        lax.rem(step_index[0], logn),
        branches,
        dest[:, :, 0],
        tokens,
        params,
        trackers,
        old_grads,
        key_weight,
        latents,
        targets,
    )


def solution(mesh):
    in_specs = (
        P(),
        P(None, "dp", None),
        P(None, "dp", None),
        P("dp", None),
        P("dp", None),
        P("dp", None),
        P(),
        P(),
        P("dp", None),
    )
    out_specs = (P("dp", None), P("dp", None))
    return jax.shard_map(shards, mesh=mesh, in_specs=in_specs, out_specs=out_specs, check_vma=False)
```

```python
from functools import partial

import jax
import jax.numpy as jnp
from jax import lax
from jax.experimental import pallas as pl
from jax.experimental.pallas import tpu as pltpu
from jax.sharding import PartitionSpec as P

HEADS = 16
STEPS = 2
GROUPS = (4, 4, 4, 4)
ATTN_HEADS = 4
F32 = jnp.float32
BF16 = jnp.bfloat16


WHOLE = pl.BlockSpec(memory_space=pltpu.VMEM)


class Chain:
    def __init__(self):
        self.token = None
        self.held = []

    def hold(self, value):
        self.held.append(value)

    def call(self, body, name, grid, ins, outs, vmem, aliases=None, scratch=(), flops=1):
        after = self.held + ([] if self.token is None else [self.token])
        self.held = []
        arrays = [a for a, _ in ins] + after
        specs = [s for _, s in ins] + [pl.BlockSpec(memory_space=pl.ANY)] * len(after)
        count_in, count_out = len(ins), len(outs)

        def kernel(*refs):
            given_out = len(arrays) + count_out
            body(*refs[:count_in], *refs[len(arrays) : given_out], *refs[given_out + 1 :])

        given = pl.pallas_call(
            kernel,
            out_shape=tuple(o for o, _ in outs) + (jax.ShapeDtypeStruct((8, 128), F32),),
            grid=grid,
            scratch_shapes=list(scratch),
            in_specs=specs,
            out_specs=tuple(s for _, s in outs) + (pl.BlockSpec(memory_space=pl.ANY),),
            input_output_aliases=dict(aliases or {}),
            compiler_params=pltpu.CompilerParams(vmem_limit_bytes=vmem * 1024 * 1024),
            cost_estimate=pl.CostEstimate(flops=flops, bytes_accessed=1, transcendentals=0),
            name=name,
        )(*arrays)
        self.token = given[-1]
        return given[:-1]


BLOCK = 256
HALF_BLOCK = 128
STRIP = 32
EARLY = 10**11


def at_block(i, size):
    return pl.ds(pl.multiple_of(i * size, size), size)


def block_of(ref, rows):
    return ref if ref.shape[0] == rows else ref.at[at_block(pl.program_id(0), rows), :]


def in_strips(body, *refs):
    flat = [ref.at[0] if len(ref.shape) == 3 else ref for ref in refs]
    rows = min(ref.shape[0] for ref in flat)
    flat = [block_of(ref, rows) for ref in flat]

    @pl.loop(0, rows // STRIP)
    def _(i):
        body(*[ref.at[at_block(i, STRIP), :] for ref in flat])


def shape(dims, dtype):
    return jax.ShapeDtypeStruct(dims, dtype)


def pack_body(dest_ref, tokens_ref, out_ref, *, count_dev, cap):
    owner = dest_ref[0]
    rows = owner.shape[1]
    trainer = lax.broadcasted_iota(jnp.int32, (count_dev, rows), 0)
    named = (trainer == owner).astype(F32)
    earlier = lax.broadcasted_iota(jnp.int32, (rows, rows), 0) < lax.broadcasted_iota(
        jnp.int32, (rows, rows), 1
    )
    before = jnp.dot(
        named.astype(BF16), earlier.astype(F32).astype(BF16), preferred_element_type=F32
    )
    rank = jnp.sum(named * before, axis=0, keepdims=True).astype(jnp.int32)
    where = owner * cap + rank

    @pl.loop(0, out_ref.shape[0] // BLOCK)
    def _(i):
        slot = lax.broadcasted_iota(jnp.int32, (BLOCK, rows), 0) + i * BLOCK
        chosen = (slot == where).astype(F32).astype(BF16)
        out_ref[at_block(i, BLOCK), :] = jnp.dot(
            chosen, tokens_ref[0], preferred_element_type=F32
        ).astype(BF16)


def pack_rows(chain, dest, tokens, count_dev):
    steps, rows, width = tokens.shape
    cap = 2 * rows // count_dev
    slots = count_dev * cap
    span = width
    return chain.call(
        partial(pack_body, count_dev=count_dev, cap=cap),
        "pack_rows",
        (steps, width // span),
        [
            (dest.reshape(steps, 1, rows), pl.BlockSpec((1, 1, rows), lambda k, i: (k, 0, 0))),
            (tokens, pl.BlockSpec((1, rows, span), lambda k, i: (k, 0, i))),
        ],
        [
            (
                pltpu.HBM((slots, steps * width), BF16),
                pl.BlockSpec((slots, span), lambda k, i: (0, k * (width // span) + i)),
            )
        ],
        vmem=16,
    )[0]


def round_body(*refs):
    def strip(src_ref, out_ref):
        out_ref[...] = src_ref[...].astype(BF16)

    in_strips(strip, *refs)


def round_columns(chain, whole, at, span, block_rows=256):
    rows = whole.shape[0]
    return chain.call(
        round_body,
        "round_columns",
        (rows // block_rows,),
        [(whole, pl.BlockSpec((block_rows, span), lambda i: (i, at)))],
        [(shape((rows, span), BF16), WHOLE)],
        vmem=4,
    )[0]


def of_head(head, head_size, value):
    column = lax.broadcasted_iota(jnp.int32, value.shape, 1) // head_size
    return jnp.where(column == head, value, 0.0)


def attn_body(rows_ref, key_ref, lat_ref, attn_ref, turned_ref, *, heads, head_size):
    @pl.when(pl.program_id(1) == 0)
    def _():
        @pl.loop(0, rows_ref.shape[0] // HALF_BLOCK)
        def _(j):
            turned_ref[0, :, at_block(j, HALF_BLOCK)] = rows_ref[at_block(j, HALF_BLOCK), :].T

    latents = lat_ref[...].astype(F32)
    queries = jnp.concatenate(
        [of_head(h, head_size, latents).astype(BF16) for h in range(heads)], axis=0
    )

    @pl.loop(0, rows_ref.shape[0] // BLOCK)
    def _(j):
        keys = jnp.dot(
            rows_ref[at_block(j, BLOCK), :], key_ref[...], preferred_element_type=F32
        ).astype(BF16)
        scores = lax.dot_general(
            queries, keys, (((1,), (1,)), ((), ())), preferred_element_type=F32
        )
        scores = scores * (1.0 / head_size**0.5) - 3.5
        attn_ref[0, :, at_block(j, BLOCK)] = jax.nn.sigmoid(scores).astype(BF16)


def attention(chain, rows, key_weight, latents, steps):
    win = rows.shape[0]
    lat, width = latents.shape
    head_size = width // HEADS
    span = ATTN_HEADS * head_size
    return chain.call(
        partial(attn_body, heads=ATTN_HEADS, head_size=head_size),
        "attention",
        (len(steps), HEADS // ATTN_HEADS),
        [
            (rows, pl.BlockSpec((win, width), lambda k, c: (0, steps[0] + k))),
            (key_weight, pl.BlockSpec((width, span), lambda k, c: (0, c))),
            (latents, pl.BlockSpec((lat, span), lambda k, c: (0, c))),
        ],
        [
            (
                shape((len(steps), HEADS * lat, win), BF16),
                pl.BlockSpec((1, ATTN_HEADS * lat, win), lambda k, c: (k, c, 0)),
            ),
            (
                shape((len(steps), width, win), BF16),
                pl.BlockSpec((1, width, win), lambda k, c: (k, 0, 0)),
            ),
        ],
        vmem=16,
    )


def grad_body(*refs, step, where, starts, heads, head_size, last):
    count = len(starts)
    rows_ref, turned_ref, attn_ref, target_ref = refs[:4]
    weight_refs = refs[4 : 4 + count]
    extra = refs[4 + count : -5]
    out_ref, weight, total, resid, dvalues = refs[-5:]
    lat = resid.shape[0] // heads
    width = weight.shape[0]
    now = pl.program_id(0)
    begin = starts[0] + now * heads

    for t in range(count):

        @pl.when(now == t)
        def _(t=t):
            @pl.loop(0, width // STRIP)
            def _(i):
                weight[at_block(i, STRIP), :] = weight_refs[t][at_block(i, STRIP), :]

    total[...] = jnp.zeros(total.shape, F32)

    @pl.loop(0, width // BLOCK)
    def _(i):
        total[...] += jnp.dot(
            rows_ref[:, at_block(step * (width // BLOCK) + i, BLOCK)],
            weight[at_block(i, BLOCK), :],
            preferred_element_type=F32,
        )

    values = total[...].astype(BF16)
    attn = attn_ref[where, at_block(begin // heads, heads * lat), :]
    out = jnp.dot(attn, values, preferred_element_type=F32)
    target = target_ref[...]
    for h in range(heads):
        part = (out[h * lat : (h + 1) * lat, :] - target) * 0.0625
        resid[h * lat : (h + 1) * lat, :] = of_head(h, head_size, part).astype(BF16)

    @pl.loop(0, dvalues.shape[0] // BLOCK)
    def _(j):
        dvalues[at_block(j, BLOCK), :] = lax.dot_general(
            attn_ref[where, at_block(begin // heads, heads * lat), at_block(j, BLOCK)],
            resid[...],
            (((0,), (0,)), ((), ())),
            preferred_element_type=F32,
        ).astype(BF16)

    @pl.loop(0, width // BLOCK)
    def _(i):
        at = at_block(i, BLOCK)
        new = jnp.dot(turned_ref[where, at, :], dvalues[...], preferred_element_type=F32)
        if last:
            grad_ref, track_ref = extra[:2]
            new = 0.5 * track_ref[0, at, :] + new - grad_ref[0, at, :]
        out_ref[0, at, :] = new


def gradient(chain, rows, attended, targets, step, some, weights, whole, extra=()):
    lat, width = targets.shape
    head_size = width // HEADS
    span = weights[0].shape[1]
    group = span // head_size
    first = some[0]
    attn, turned, where = attended
    each = pl.BlockSpec((1, width, span), lambda t: (first + t, 0, 0))
    ins = [
        (rows, WHOLE),
        (turned, WHOLE),
        (attn, WHOLE),
        (targets, pl.BlockSpec((lat, span), lambda t: (0, first + t))),
    ]
    ins += [(a, WHOLE) for a in weights] + [(a, each) for a in extra]
    aliases = {}
    if whole is not None:
        aliases = {len(ins): 0}
        ins.append((whole, pl.BlockSpec(memory_space=pl.ANY)))
    return chain.call(
        partial(
            grad_body,
            step=step,
            where=where,
            starts=[group * i for i in some],
            heads=group,
            head_size=head_size,
            last=bool(extra),
        ),
        "gradient",
        (len(some),),
        ins,
        [(shape((HEADS // group, width, span), F32), each)],
        vmem=20,
        aliases=aliases,
        scratch=[
            pltpu.VMEM((width, span), BF16),
            pltpu.VMEM((rows.shape[0], span), F32),
            pltpu.VMEM((group * lat, span), BF16),
            pltpu.VMEM((rows.shape[0], span), BF16),
        ],
    )[0]


def mix_body(*refs):
    def strip(weight_ref, track_ref, got_ref, new_ref, sent_ref):
        new = 0.5 * (weight_ref[...] + got_ref[...].astype(F32)) - 0.05 * track_ref[...]
        new_ref[...] = new
        sent_ref[...] = new.astype(BF16)

    in_strips(strip, *refs)


def mix_weight(chain, weight, track, got, at, flops, block_rows=256):
    rows, span = got.shape
    wide = pl.BlockSpec((block_rows, span), lambda i: (i, at))
    return chain.call(
        mix_body,
        "mix_weight",
        (rows // block_rows,),
        [(weight, wide), (track, wide), (got, WHOLE)],
        [(shape((rows, span), F32), WHOLE), (shape((rows, span), BF16), WHOLE)],
        vmem=8,
        flops=flops,
    )


def update_body(*refs):
    def strip(track, track_got, grad, old, weight, weight_got, track_out, track_sent, weight_out, weight_used):
        new_track = 0.5 * (track[...] + track_got[...].astype(F32)) + grad[...] - old[...]
        track_out[...] = new_track
        track_sent[...] = new_track.astype(BF16)
        new_weight = 0.5 * (weight[...] + weight_got[...].astype(F32)) - 0.05 * new_track
        weight_out[...] = new_weight
        weight_used[...] = new_weight.astype(BF16)

    in_strips(strip, *refs[:6], *refs[-4:])


def update(chain, trackers, track_got, grad, old, weight, weight_got, wholes, at, part, block_rows=256):
    rows, span = weight.shape
    width = trackers.shape[1]
    wide = pl.BlockSpec((block_rows, span), lambda i: (i, at))
    mine = pl.BlockSpec((1, block_rows, span), lambda i: (part, i, 0))
    ins = [
        (trackers, wide),
        (track_got, WHOLE),
        (grad, mine),
        (old, wide),
        (weight, WHOLE),
        (weight_got, WHOLE),
    ]
    aliases = {}
    for out, whole in zip((0, 2), wholes):
        if whole is not None:
            aliases[len(ins)] = out
            ins.append((whole, pl.BlockSpec(memory_space=pl.ANY)))
    return chain.call(
        update_body,
        "update",
        (rows // block_rows,),
        ins,
        [
            (shape(grad.shape, F32), mine),
            (shape((rows, span), BF16), WHOLE),
            (pltpu.HBM((rows, width), F32), wide),
            (shape((rows, span), BF16), WHOLE),
        ],
        vmem=12,
        aliases=aliases,
    )


def place_body(*refs, count):
    part_ref, out_ref = refs[0], refs[-1]
    got_refs = [block_of(ref, out_ref.shape[0]) for ref in refs[1 : 1 + count]]
    span = got_refs[0].shape[1]

    @pl.loop(0, out_ref.shape[0] // STRIP)
    def _(i):
        at = at_block(i, STRIP)
        for t in range(count):
            out_ref[at, t * span : (t + 1) * span] = part_ref[t, at, :] + 0.5 * got_refs[t][
                at, :
            ].astype(F32)


def place(chain, part, gots, whole, first, width, block_rows=256):
    rows, span = gots[0].shape
    count = len(gots)
    ins = [(part, pl.BlockSpec((count, block_rows, span), lambda i: (first // count, i, 0)))]
    ins += [(got, WHOLE) for got in gots]
    aliases = {}
    if whole is not None:
        aliases = {len(ins): 0}
        ins.append((whole, pl.BlockSpec(memory_space=pl.ANY)))
    return chain.call(
        partial(place_body, count=count),
        "place",
        (rows // block_rows,),
        ins,
        [
            (
                pltpu.HBM((rows, width), F32),
                pl.BlockSpec((block_rows, count * span), lambda i: (i, first // count)),
            )
        ],
        vmem=12,
        aliases=aliases,
    )[0]


def from_partner(value, bit):
    size = lax.axis_size("dp")
    return lax.ppermute(value, "dp", [(s, s ^ (1 << bit)) for s in range(size)])


def exchange_rows(packed, count_dev):
    slots, width = packed.shape
    blocks = packed.reshape(count_dev, slots // count_dev, width)
    got = lax.all_to_all(blocks, "dp", split_axis=0, concat_axis=0, tiled=True)
    return got.reshape(slots, width)


def plan(bits, top, count):
    first, second = bits
    last = count - 1
    cut = count // 2
    apart = top not in bits
    if first == 0:
        order = [("pack", 0), ("send", 0), ("send", 1), ("send", 2)]
    else:
        order = [("send", 0), ("send", 1), ("pack", 0)]
    for c in range(count):
        order += [("hold_x", c - 2), ("mix" if first == 0 or c else "mix_late", c)]
        order += [("send", 2)] if c == 0 and first != 0 else []
        order += [("send", c + 3)]
        if c == count // 2 and first != 0:
            order += [("attn", 0 if apart else 2)]
    order += [("attn", 0 if apart else 2)] if first == 0 else []
    late = apart and first != 0
    order += [("grad", 0), ("hold_x", count - 2)] if late else [("hold_x", count - 2), ("grad", 0)]
    for c in range(count):
        if c == cut:
            order += [("grad", 1), ("hold_x", last)]
        order += [("hold_y", c - 2), ("update", c), ("send", count + 3 + c)]
        order += [("attn", 1)] if apart and c == 0 else []
        if second == 0 and c == cut - 1:
            order += [("final", 0)]
        if second == 0 and c == cut:
            order += [("place", 0)]
    if second == 0:
        return cut, cut, order + [("final", 1), ("place", 1)]
    return cut, last, order + [("final", 2), ("place", 0), ("place", 1)]


def two_steps(dest, tokens, params, trackers, old_grads, key_weight, latents, targets, *, bits):
    count_dev = lax.axis_size("dp")
    width = params.shape[1]
    head_size = width // HEADS
    count = len(GROUPS)
    spans = [g * head_size for g in GROUPS]
    starts = [sum(GROUPS[:c]) for c in range(count)]
    at = [s // g for s, g in zip(starts, GROUPS)]
    first, second = bits

    chain = Chain()
    got0, x1, x1b, x1_got, x2b, y1_got = {}, {}, {}, {}, {}, {}
    attended = {}
    rows = g1 = y1 = part = new_params = new_trackers = None
    cut, split, order = plan(bits, count_dev.bit_length() - 2, count)
    for what, c in order:
        if what == "pack":
            rows = exchange_rows(pack_rows(chain, dest, tokens, count_dev), count_dev)
        elif what == "send" and c < 2 * count:
            whole, i = (params, c) if c < count else (trackers, c - count)
            got0[c] = from_partner(round_columns(chain, whole, at[i], spans[i]), first)
        elif what == "hold_x" and c >= 0:
            chain.hold(x1_got[c])
        elif what == "hold_y" and c >= 0:
            chain.hold(y1_got[c])
        elif what in ("mix", "mix_late"):
            x1[c], x1b[c] = mix_weight(
                chain, params, trackers, got0[c], at[c], EARLY if what == "mix_late" else 1
            )
            x1_got[c] = from_partner(x1b[c], second)
        elif what == "attn":
            steps = (range(1), range(1, STEPS), range(STEPS))[c]
            given = attention(chain, rows, key_weight, latents, steps)
            attended |= {step: (*given, step - steps[0]) for step in steps}
        elif what == "grad":
            some = range(cut, count) if c else range(cut)
            g1 = gradient(chain, rows, attended[0], targets, 0, some, [x1b[i] for i in some], g1)
        elif what == "final":
            some = (range(cut), range(cut, count), range(count))[c]
            part = gradient(
                chain, rows, attended[1], targets, 1, some, [x2b[i] for i in some], part, (g1, y1)
            )
        elif what == "update":
            y1, sent, new_params, x2b[c] = update(
                chain,
                trackers,
                got0[count + c],
                g1,
                old_grads,
                x1[c],
                x1_got[c],
                (y1, new_params),
                at[c],
                c,
            )
            y1_got[c] = from_partner(sent, second)
        elif what == "place":
            some = range(split, count) if c else range(split)
            new_trackers = place(
                chain, part, [y1_got[i] for i in some], new_trackers, some[0], width
            )
    return new_params, new_trackers


def shards(step_index, dest, tokens, params, trackers, old_grads, key_weight, latents, targets):
    logn = lax.axis_size("dp").bit_length() - 1
    branches = [partial(two_steps, bits=(b, (b + 1) % logn)) for b in range(logn)]
    return lax.switch(
        lax.rem(step_index[0], logn),
        branches,
        dest[:, :, 0],
        tokens,
        params,
        trackers,
        old_grads,
        key_weight,
        latents,
        targets,
    )


def solution(mesh):
    in_specs = (
        P(),
        P(None, "dp", None),
        P(None, "dp", None),
        P("dp", None),
        P("dp", None),
        P("dp", None),
        P(),
        P(),
        P("dp", None),
    )
    out_specs = (P("dp", None), P("dp", None))
    return jax.shard_map(shards, mesh=mesh, in_specs=in_specs, out_specs=out_specs, check_vma=False)
```

```python
from functools import partial

import jax
import jax.numpy as jnp
from jax import lax
from jax.experimental import pallas as pl
from jax.experimental.pallas import tpu as pltpu
from jax.sharding import PartitionSpec as P

HEADS = 16
STEPS = 2
GROUPS = (4, 4, 4, 4)
ATTN_HEADS = 4
F32 = jnp.float32
BF16 = jnp.bfloat16


WHOLE = pl.BlockSpec(memory_space=pltpu.VMEM)


class Chain:
    def __init__(self):
        self.token = None
        self.held = []

    def hold(self, value):
        self.held.append(value)

    def call(self, body, name, grid, ins, outs, vmem, aliases=None, scratch=(), flops=1):
        after = self.held + ([] if self.token is None else [self.token])
        self.held = []
        arrays = [a for a, _ in ins] + after
        specs = [s for _, s in ins] + [pl.BlockSpec(memory_space=pl.ANY)] * len(after)
        count_in, count_out = len(ins), len(outs)

        def kernel(*refs):
            given_out = len(arrays) + count_out
            body(*refs[:count_in], *refs[len(arrays) : given_out], *refs[given_out + 1 :])

        given = pl.pallas_call(
            kernel,
            out_shape=tuple(o for o, _ in outs) + (jax.ShapeDtypeStruct((8, 128), F32),),
            grid=grid,
            scratch_shapes=list(scratch),
            in_specs=specs,
            out_specs=tuple(s for _, s in outs) + (pl.BlockSpec(memory_space=pl.ANY),),
            input_output_aliases=dict(aliases or {}),
            compiler_params=pltpu.CompilerParams(vmem_limit_bytes=vmem * 1024 * 1024),
            cost_estimate=pl.CostEstimate(flops=flops, bytes_accessed=1, transcendentals=0),
            name=name,
        )(*arrays)
        self.token = given[-1]
        return given[:-1]


BLOCK = 256
HALF_BLOCK = 128
STRIP = 32
EARLY = 10**11


def at_block(i, size):
    return pl.ds(pl.multiple_of(i * size, size), size)


def block_of(ref, rows):
    return ref if ref.shape[0] == rows else ref.at[at_block(pl.program_id(0), rows), :]


def in_strips(body, *refs):
    flat = [ref.at[0] if len(ref.shape) == 3 else ref for ref in refs]
    rows = min(ref.shape[0] for ref in flat)
    flat = [block_of(ref, rows) for ref in flat]

    @pl.loop(0, rows // STRIP)
    def _(i):
        body(*[ref.at[at_block(i, STRIP), :] for ref in flat])


def shape(dims, dtype):
    return jax.ShapeDtypeStruct(dims, dtype)


def pack_body(dest_ref, tokens_ref, out_ref, *, count_dev, cap):
    owner = dest_ref[0]
    rows = owner.shape[1]
    trainer = lax.broadcasted_iota(jnp.int32, (count_dev, rows), 0)
    named = (trainer == owner).astype(F32)
    earlier = lax.broadcasted_iota(jnp.int32, (rows, rows), 0) < lax.broadcasted_iota(
        jnp.int32, (rows, rows), 1
    )
    before = jnp.dot(
        named.astype(BF16), earlier.astype(F32).astype(BF16), preferred_element_type=F32
    )
    rank = jnp.sum(named * before, axis=0, keepdims=True).astype(jnp.int32)
    where = owner * cap + rank

    @pl.loop(0, out_ref.shape[0] // BLOCK)
    def _(i):
        slot = lax.broadcasted_iota(jnp.int32, (BLOCK, rows), 0) + i * BLOCK
        chosen = (slot == where).astype(F32).astype(BF16)
        out_ref[at_block(i, BLOCK), :] = jnp.dot(
            chosen, tokens_ref[0], preferred_element_type=F32
        ).astype(BF16)


def pack_rows(chain, dest, tokens, count_dev):
    steps, rows, width = tokens.shape
    cap = 2 * rows // count_dev
    slots = count_dev * cap
    span = width
    return chain.call(
        partial(pack_body, count_dev=count_dev, cap=cap),
        "pack_rows",
        (steps, width // span),
        [
            (dest.reshape(steps, 1, rows), pl.BlockSpec((1, 1, rows), lambda k, i: (k, 0, 0))),
            (tokens, pl.BlockSpec((1, rows, span), lambda k, i: (k, 0, i))),
        ],
        [
            (
                pltpu.HBM((slots, steps * width), BF16),
                pl.BlockSpec((slots, span), lambda k, i: (0, k * (width // span) + i)),
            )
        ],
        vmem=16,
    )[0]


def round_body(*refs):
    def strip(src_ref, out_ref):
        out_ref[...] = src_ref[...].astype(BF16)

    in_strips(strip, *refs)


def round_columns(chain, whole, at, span, block_rows=256):
    rows = whole.shape[0]
    return chain.call(
        round_body,
        "round_columns",
        (rows // block_rows,),
        [(whole, pl.BlockSpec((block_rows, span), lambda i: (i, at)))],
        [(shape((rows, span), BF16), WHOLE)],
        vmem=4,
    )[0]


def of_head(head, head_size, value):
    column = lax.broadcasted_iota(jnp.int32, value.shape, 1) // head_size
    return jnp.where(column == head, value, 0.0)


def attn_body(rows_ref, key_ref, lat_ref, attn_ref, turned_ref, *, heads, head_size):
    @pl.when(pl.program_id(1) == 0)
    def _():
        @pl.loop(0, rows_ref.shape[0] // HALF_BLOCK)
        def _(j):
            turned_ref[0, :, at_block(j, HALF_BLOCK)] = rows_ref[at_block(j, HALF_BLOCK), :].T

    latents = lat_ref[...].astype(F32)
    queries = jnp.concatenate(
        [of_head(h, head_size, latents).astype(BF16) for h in range(heads)], axis=0
    )

    @pl.loop(0, rows_ref.shape[0] // BLOCK)
    def _(j):
        keys = jnp.dot(
            rows_ref[at_block(j, BLOCK), :], key_ref[...], preferred_element_type=F32
        ).astype(BF16)
        scores = lax.dot_general(
            queries, keys, (((1,), (1,)), ((), ())), preferred_element_type=F32
        )
        scores = scores * (1.0 / head_size**0.5) - 3.5
        attn_ref[0, :, at_block(j, BLOCK)] = jax.nn.sigmoid(scores).astype(BF16)


def attention(chain, rows, key_weight, latents, steps):
    win = rows.shape[0]
    lat, width = latents.shape
    head_size = width // HEADS
    span = ATTN_HEADS * head_size
    return chain.call(
        partial(attn_body, heads=ATTN_HEADS, head_size=head_size),
        "attention",
        (len(steps), HEADS // ATTN_HEADS),
        [
            (rows, pl.BlockSpec((win, width), lambda k, c: (0, steps[0] + k))),
            (key_weight, pl.BlockSpec((width, span), lambda k, c: (0, c))),
            (latents, pl.BlockSpec((lat, span), lambda k, c: (0, c))),
        ],
        [
            (
                shape((len(steps), HEADS * lat, win), BF16),
                pl.BlockSpec((1, ATTN_HEADS * lat, win), lambda k, c: (k, c, 0)),
            ),
            (
                shape((len(steps), width, win), BF16),
                pl.BlockSpec((1, width, win), lambda k, c: (k, 0, 0)),
            ),
        ],
        vmem=16,
    )


def grad_body(*refs, step, where, starts, heads, head_size, last):
    count = len(starts)
    rows_ref, turned_ref, attn_ref, target_ref = refs[:4]
    weight_refs = refs[4 : 4 + count]
    extra = refs[4 + count : -5]
    out_ref, weight, total, resid, dvalues = refs[-5:]
    lat = resid.shape[0] // heads
    width = weight.shape[0]
    now = pl.program_id(0)
    begin = starts[0] + now * heads

    for t in range(count):

        @pl.when(now == t)
        def _(t=t):
            @pl.loop(0, width // STRIP)
            def _(i):
                weight[at_block(i, STRIP), :] = weight_refs[t][at_block(i, STRIP), :]

    total[...] = jnp.zeros(total.shape, F32)

    @pl.loop(0, width // BLOCK)
    def _(i):
        total[...] += jnp.dot(
            rows_ref[:, at_block(step * (width // BLOCK) + i, BLOCK)],
            weight[at_block(i, BLOCK), :],
            preferred_element_type=F32,
        )

    values = total[...].astype(BF16)
    attn = attn_ref[where, at_block(begin // heads, heads * lat), :]
    out = jnp.dot(attn, values, preferred_element_type=F32)
    target = target_ref[...]
    for h in range(heads):
        part = (out[h * lat : (h + 1) * lat, :] - target) * 0.0625
        resid[h * lat : (h + 1) * lat, :] = of_head(h, head_size, part).astype(BF16)

    @pl.loop(0, dvalues.shape[0] // BLOCK)
    def _(j):
        dvalues[at_block(j, BLOCK), :] = lax.dot_general(
            attn_ref[where, at_block(begin // heads, heads * lat), at_block(j, BLOCK)],
            resid[...],
            (((0,), (0,)), ((), ())),
            preferred_element_type=F32,
        ).astype(BF16)

    @pl.loop(0, width // BLOCK)
    def _(i):
        at = at_block(i, BLOCK)
        new = jnp.dot(turned_ref[where, at, :], dvalues[...], preferred_element_type=F32)
        if last:
            grad_ref, track_ref = extra[:2]
            new = 0.5 * track_ref[0, at, :] + new - grad_ref[0, at, :]
        out_ref[0, at, :] = new


def gradient(chain, rows, attended, targets, step, some, weights, whole, extra=()):
    lat, width = targets.shape
    head_size = width // HEADS
    span = weights[0].shape[1]
    group = span // head_size
    first = some[0]
    attn, turned, where = attended
    each = pl.BlockSpec((1, width, span), lambda t: (first + t, 0, 0))
    ins = [
        (rows, WHOLE),
        (turned, WHOLE),
        (attn, WHOLE),
        (targets, pl.BlockSpec((lat, span), lambda t: (0, first + t))),
    ]
    ins += [(a, WHOLE) for a in weights] + [(a, each) for a in extra]
    aliases = {}
    if whole is not None:
        aliases = {len(ins): 0}
        ins.append((whole, pl.BlockSpec(memory_space=pl.ANY)))
    return chain.call(
        partial(
            grad_body,
            step=step,
            where=where,
            starts=[group * i for i in some],
            heads=group,
            head_size=head_size,
            last=bool(extra),
        ),
        "gradient",
        (len(some),),
        ins,
        [(shape((HEADS // group, width, span), F32), each)],
        vmem=20,
        aliases=aliases,
        scratch=[
            pltpu.VMEM((width, span), BF16),
            pltpu.VMEM((rows.shape[0], span), F32),
            pltpu.VMEM((group * lat, span), BF16),
            pltpu.VMEM((rows.shape[0], span), BF16),
        ],
    )[0]


def mix_body(*refs):
    def strip(weight_ref, track_ref, got_ref, new_ref, sent_ref):
        new = 0.5 * (weight_ref[...] + got_ref[...].astype(F32)) - 0.05 * track_ref[...]
        new_ref[...] = new
        sent_ref[...] = new.astype(BF16)

    in_strips(strip, *refs)


def mix_weight(chain, weight, track, got, at, flops, block_rows=256):
    rows, span = got.shape
    wide = pl.BlockSpec((block_rows, span), lambda i: (i, at))
    return chain.call(
        mix_body,
        "mix_weight",
        (rows // block_rows,),
        [(weight, wide), (track, wide), (got, WHOLE)],
        [(shape((rows, span), F32), WHOLE), (shape((rows, span), BF16), WHOLE)],
        vmem=8,
        flops=flops,
    )


def update_body(*refs):
    def strip(track, track_got, grad, old, weight, weight_got, track_out, track_sent, weight_out, weight_used):
        new_track = 0.5 * (track[...] + track_got[...].astype(F32)) + grad[...] - old[...]
        track_out[...] = new_track
        track_sent[...] = new_track.astype(BF16)
        new_weight = 0.5 * (weight[...] + weight_got[...].astype(F32)) - 0.05 * new_track
        weight_out[...] = new_weight
        weight_used[...] = new_weight.astype(BF16)

    in_strips(strip, *refs[:6], *refs[-4:])


def update(chain, trackers, track_got, grad, old, weight, weight_got, wholes, at, part, block_rows=256):
    rows, span = weight.shape
    width = trackers.shape[1]
    wide = pl.BlockSpec((block_rows, span), lambda i: (i, at))
    mine = pl.BlockSpec((1, block_rows, span), lambda i: (part, i, 0))
    ins = [
        (trackers, wide),
        (track_got, WHOLE),
        (grad, mine),
        (old, wide),
        (weight, WHOLE),
        (weight_got, WHOLE),
    ]
    aliases = {}
    for out, whole in zip((0, 2), wholes):
        if whole is not None:
            aliases[len(ins)] = out
            ins.append((whole, pl.BlockSpec(memory_space=pl.ANY)))
    return chain.call(
        update_body,
        "update",
        (rows // block_rows,),
        ins,
        [
            (shape(grad.shape, F32), mine),
            (shape((rows, span), BF16), WHOLE),
            (pltpu.HBM((rows, width), F32), wide),
            (shape((rows, span), BF16), WHOLE),
        ],
        vmem=12,
        aliases=aliases,
    )


def place_body(*refs, count):
    part_ref, out_ref = refs[0], refs[-1]
    got_refs = [block_of(ref, out_ref.shape[0]) for ref in refs[1 : 1 + count]]
    span = got_refs[0].shape[1]

    @pl.loop(0, out_ref.shape[0] // STRIP)
    def _(i):
        at = at_block(i, STRIP)
        for t in range(count):
            out_ref[at, t * span : (t + 1) * span] = part_ref[t, at, :] + 0.5 * got_refs[t][
                at, :
            ].astype(F32)


def place(chain, part, gots, whole, first, width, block_rows=256):
    rows, span = gots[0].shape
    count = len(gots)
    ins = [(part, pl.BlockSpec((count, block_rows, span), lambda i: (first // count, i, 0)))]
    ins += [(got, WHOLE) for got in gots]
    aliases = {}
    if whole is not None:
        aliases = {len(ins): 0}
        ins.append((whole, pl.BlockSpec(memory_space=pl.ANY)))
    return chain.call(
        partial(place_body, count=count),
        "place",
        (rows // block_rows,),
        ins,
        [
            (
                pltpu.HBM((rows, width), F32),
                pl.BlockSpec((block_rows, count * span), lambda i: (i, first // count)),
            )
        ],
        vmem=12,
        aliases=aliases,
    )[0]


def from_partner(value, bit):
    size = lax.axis_size("dp")
    return lax.ppermute(value, "dp", [(s, s ^ (1 << bit)) for s in range(size)])


def exchange_rows(packed, count_dev):
    slots, width = packed.shape
    blocks = packed.reshape(count_dev, slots // count_dev, width)
    got = lax.all_to_all(blocks, "dp", split_axis=0, concat_axis=0, tiled=True)
    return got.reshape(slots, width)


def plan(bits, top, count):
    first, second = bits
    last = count - 1
    cut = count // 2
    apart = top not in bits
    if first == 0:
        order = [("pack", 0), ("send", 0), ("send", 1), ("send", 2)]
    else:
        order = [("send", 0), ("send", 1), ("pack", 0)]
    for c in range(count):
        order += [("hold_x", c - 2), ("mix" if first == 0 or c else "mix_late", c)]
        order += [("send", 2)] if c == 0 and first != 0 else []
        order += [] if apart and first != 0 and c == last else [("send", c + 3)]
        if c == count // 2 and first != 0:
            order += [("attn", 0 if apart else 2)]
    order += [("attn", 0 if apart else 2)] if first == 0 else []
    late = apart and first != 0
    order += [("grad", 0), ("hold_x", count - 2)] if late else [("hold_x", count - 2), ("grad", 0)]
    for c in range(count):
        if c == cut:
            order += [("grad", 1), ("hold_x", last)]
        order += [("hold_y", c - 2), ("update", c)]
        order += [("attn", 1)] if apart and c == 0 else []
        order += [("send", count + c + (2 if late else 3))]
        order += [("final", 0)] if late and c == cut else []
        if second == 0 and c == cut - 1:
            order += [("final", 0)]
        if second == 0 and c == cut:
            order += [("final", 3), ("place", 0)]
    if second == 0:
        return cut, cut, order + [("final", 4), ("place", 1)]
    return cut, last, order + [("final", 1 if late else 2), ("place", 0), ("place", 1)]


def two_steps(dest, tokens, params, trackers, old_grads, key_weight, latents, targets, *, bits):
    count_dev = lax.axis_size("dp")
    width = params.shape[1]
    head_size = width // HEADS
    count = len(GROUPS)
    spans = [g * head_size for g in GROUPS]
    starts = [sum(GROUPS[:c]) for c in range(count)]
    at = [s // g for s, g in zip(starts, GROUPS)]
    first, second = bits

    chain = Chain()
    got0, x1, x1b, x1_got, x2b, y1_got = {}, {}, {}, {}, {}, {}
    attended = {}
    rows = g1 = y1 = part = new_params = new_trackers = None
    cut, split, order = plan(bits, count_dev.bit_length() - 2, count)
    for what, c in order:
        if what == "pack":
            rows = exchange_rows(pack_rows(chain, dest, tokens, count_dev), count_dev)
        elif what == "send" and c < 2 * count:
            whole, i = (params, c) if c < count else (trackers, c - count)
            got0[c] = from_partner(round_columns(chain, whole, at[i], spans[i]), first)
        elif what == "hold_x" and c >= 0:
            chain.hold(x1_got[c])
        elif what == "hold_y" and c >= 0:
            chain.hold(y1_got[c])
        elif what in ("mix", "mix_late"):
            x1[c], x1b[c] = mix_weight(
                chain, params, trackers, got0[c], at[c], EARLY if what == "mix_late" else 1
            )
            x1_got[c] = from_partner(x1b[c], second)
        elif what == "attn":
            steps = (range(1), range(1, STEPS), range(STEPS))[c]
            given = attention(chain, rows, key_weight, latents, steps)
            attended |= {step: (*given, step - steps[0]) for step in steps}
        elif what == "grad":
            some = range(cut, count) if c else range(cut)
            g1 = gradient(chain, rows, attended[0], targets, 0, some, [x1b[i] for i in some], g1)
        elif what == "final":
            last = count - 1
            some = (range(cut), range(cut, count), range(count), range(cut, last), range(last, count))[c]
            part = gradient(
                chain, rows, attended[1], targets, 1, some, [x2b[i] for i in some], part, (g1, y1)
            )
        elif what == "update":
            y1, sent, new_params, x2b[c] = update(
                chain,
                trackers,
                got0[count + c],
                g1,
                old_grads,
                x1[c],
                x1_got[c],
                (y1, new_params),
                at[c],
                c,
            )
            y1_got[c] = from_partner(sent, second)
        elif what == "place":
            some = range(split, count) if c else range(split)
            new_trackers = place(
                chain, part, [y1_got[i] for i in some], new_trackers, some[0], width
            )
    return new_params, new_trackers


def shards(step_index, dest, tokens, params, trackers, old_grads, key_weight, latents, targets):
    logn = lax.axis_size("dp").bit_length() - 1
    branches = [partial(two_steps, bits=(b, (b + 1) % logn)) for b in range(logn)]
    return lax.switch(
        lax.rem(step_index[0], logn),
        branches,
        dest[:, :, 0],
        tokens,
        params,
        trackers,
        old_grads,
        key_weight,
        latents,
        targets,
    )


def solution(mesh):
    in_specs = (
        P(),
        P(None, "dp", None),
        P(None, "dp", None),
        P("dp", None),
        P("dp", None),
        P("dp", None),
        P(),
        P(),
        P("dp", None),
    )
    out_specs = (P("dp", None), P("dp", None))
    return jax.shard_map(shards, mesh=mesh, in_specs=in_specs, out_specs=out_specs, check_vma=False)
```
